256 devices in a mesh: ctx: 16 (over y, x), exp: 8 (over z), half: 2 (over core).
Axes of the slice: x: 4, y: 4, z: 8, core: 2. Of those that a mesh axis runs over, the one named last changes fastest.
Arguments:
- residual: bfloat16 [2048, 4096], P(('ctx', 'exp', 'half')), may hold values from -6 to 6
- mixer_input: bfloat16 [2048, 8192], P('ctx', ('exp', 'half')), may hold values from -6 to 6
- mixer_gate: bfloat16 [2048, 8192], P('ctx', ('exp', 'half')), may hold values from -6 to 6
- step_size: float32 [2048, 8192], P('ctx', ('exp', 'half')), may hold values from 0 to 2, as said below
- decay_rate: float32 [16, 8192], P(None, ('exp', 'half')), may hold values from 0.02 to 8
- state_in: float32 [2048, 16], P('ctx'), may hold values from -6 to 6
- state_out: float32 [2048, 16], P('ctx'), may hold values from -6 to 6
- skip_weight: float32 [8192], P(('exp', 'half')), may hold values from 0.5 to 1.5
- projection: bfloat16 [8192, 4096], P(('exp', 'half')), may hold values from -0.0625 to 0.0625
- norm_gain: float32 [4096], replicated, may hold values from 0.1 to 1.9
- routes: int32 [2048, 2], P('ctx'), may hold values from 0 to 7, all different within a row; in each aligned block of 128 rows (0 to 127, 128 to 255, ...) at most 64 rows name the same one
- route_weight: float32 [2048, 2], P('ctx'), may hold values from 0.2 to 1
- up_weight: bfloat16 [8, 4096, 12288], P('exp', None, ('ctx', 'half')), may hold values from -0.09375 to 0.09375
- down_weight: bfloat16 [8, 12288, 4096], P('exp', ('ctx', 'half')), may hold values from -0.0546875 to 0.0546875
Outputs:
- mixed: bfloat16 [2048, 4096], P(('ctx', 'exp', 'half'))
The draws below stay inside these ranges and needn't reach their ends.
Inputs may be any that keep to these rules, and one draw needn't show every extreme that they name: `routes`: the two experts of a token differ. Within each block of 128 consecutive positions every expert is named by at most 64 tokens, and in some block one expert is named by exactly 64. `step_size`: Positive.
All inputs are finite; a program needn't handle non-finite values.
Results may differ from the reference program's by a relative error of at most 0.0075.
Values may be sent and summed in bfloat16 or wider, within the bound.
A program may use at most 128 MiB of HBM per device.

```python
import math
import jax
import jax.numpy as jnp
import numpy as np
from jax import lax

D = 4096
CHANNEL_SLICE = 8192
STATE = 16
FF = 12288
CTX_TOK = 128
SEQUENCE_LENGTH = 2048
EXPERTS = 8
CAP = 64
N_CTX = 16
N_HALF = 2


def draw_step_size(key, part):
    key = jax.random.fold_in(key, 7)
    baseline_seed, noisy_seed, location_seed, spike_seed = jax.random.split(key, 4)
    upper = 64.0
    unit = jax.random.uniform(baseline_seed, (CHANNEL_SLICE,), jnp.float32)
    baseline_values = jnp.exp(unit * jnp.log(upper)) / SEQUENCE_LENGTH
    noisy_values = jax.random.uniform(noisy_seed, (SEQUENCE_LENGTH, CHANNEL_SLICE), jnp.float32, 0.5, 2.0)
    spots = jax.random.randint(location_seed, (4,), 0, SEQUENCE_LENGTH)
    spike_values = jax.random.uniform(spike_seed, (SEQUENCE_LENGTH, CHANNEL_SLICE), jnp.float32, 0.5, 2.0)
    sample_location = jnp.any(jnp.arange(SEQUENCE_LENGTH)[:, None] == spots[None, :], axis=1)
    return jnp.where(sample_location[:, None], spike_values, baseline_values[None, :] * noisy_values)


def levels(rng, shape, cuts, least, high):
    def one(axis_at, shards_of):
        steps = jax.random.uniform(jax.random.fold_in(jax.random.fold_in(rng, 6), axis_at), (shards_of,), jnp.float32, least / len(cuts), high / len(cuts))
        return jnp.repeat(jnp.exp(steps), shape[axis_at] // shards_of).reshape((-1,) + (1,) * (len(shape) - axis_at - 1))

    level = one(*cuts[0])
    for cut in cuts[1:]:
        level = level * one(*cut)
    return level


def routed_block(stream_key, own, number, rows, count, top, limit, skew):
    ranking = jax.random.permutation(stream_key, count)
    heavy_load, common = portions_of(count, rows * top, limit, skew, True), portions_of(count, rows * top, limit, skew, False)
    places = jnp.arange(count)

    def named(sizes, turn):
        used = int((sizes > 0).sum())
        fixed = max(1, used // 4)
        shifted = fixed + (places - fixed + turn * (used - fixed)) % max(1, count - fixed)
        return jnp.zeros((count,), jnp.int32).at[ranking[jnp.where(places < fixed, places, shifted)]].set(jnp.asarray(sizes, jnp.int32))

    sizes = jnp.where(number % 4 == 0, named(heavy_load, number // 4), named(common, number - number // 4 - 1))
    mixed = jax.random.permutation(jax.random.fold_in(own, 3), count)
    giver, sink = mixed[0:count // 2 * 2:2], mixed[1:count // 2 * 2:2]
    slack = jnp.minimum(sizes[giver] - 1, limit - sizes[sink]) // 2
    slack = jnp.where((giver == ranking[0]) | (sink == ranking[0]) | (sizes[sink] == 0), 0, jnp.maximum(slack, 0))
    shifted = jax.random.randint(jax.random.fold_in(own, 4), (count // 2,), 0, 1 << 20) % (slack + 1)
    sizes = sizes.at[giver].add(-shifted).at[sink].add(shifted)
    labels = jnp.searchsorted(jnp.cumsum(sizes), jnp.arange(rows * top), side="right").astype(jnp.int32)
    table = labels.reshape(top, rows).T
    table = table[jax.random.permutation(jax.random.fold_in(own, 1), rows)]
    turn = jax.random.randint(jax.random.fold_in(own, 2), (rows, 1), 0, top)
    return jnp.take_along_axis(table, (jnp.arange(top)[None, :] + turn) % top, axis=1)


def portions_of(number_of, total, most, lean, full):
    portions = [(1 << 20) // math.isqrt(grade ** lean) + 1 for grade in range(1, number_of + 1)]
    largest = most if full else min(most, max(-(-total // number_of), total * portions[0] // sum(portions)))
    least = 1 if total - largest >= number_of - 1 else 0
    counts, spare = [largest] + [least] * (number_of - 1), total - largest - least * (number_of - 1)
    while spare > 0:
        candidates = [i for i in range(1, number_of) if counts[i] < largest] or [i for i in range(1, number_of) if counts[i] < most]
        mass, left = sum([portions[i] for i in candidates]), spare
        for i in candidates:
            extra = min(most - counts[i], max(1, left * portions[i] // mass), spare)
            counts[i] = counts[i] + extra
            spare = spare - extra
    return np.array(counts)


def normal_values(own_key, shape, deviation, reach, shards=(), kind=jnp.bfloat16):
    loudness = levels(own_key, shape, shards, -0.22, 0.18) if shards else 1.0
    drawn = jax.random.normal(own_key, shape, jnp.float32) * deviation * loudness
    return jnp.minimum(jnp.maximum(drawn, -reach), reach).astype(kind)


def setup_inputs(seed: int = 0) -> dict:
    keys = jax.random.split(jax.random.key(seed), 15)
    residual = normal_values(keys[0], (SEQUENCE_LENGTH, D), 1.0, 6.0, ((0, 256),))
    mixer_input = normal_values(keys[1], (SEQUENCE_LENGTH, CHANNEL_SLICE), 1.0, 6.0, ((0, 16), (1, 16)))
    mixer_gate = normal_values(keys[2], (SEQUENCE_LENGTH, CHANNEL_SLICE), 1.0, 6.0, ((0, 16), (1, 16)))
    step_size = draw_step_size(jax.random.fold_in(keys[14], 71), 0)
    decay_rate = jnp.clip(jnp.exp(math.log(8.0) - 5.9914646 * jax.random.uniform(keys[4], (STATE, CHANNEL_SLICE), jnp.float32) ** levels(keys[4], (STATE, CHANNEL_SLICE), ((1, 16),), -0.2, 0.2)), 0.02, 8.0)
    state_in = normal_values(keys[5], (SEQUENCE_LENGTH, STATE), 1.0, 6.0, ((0, 16),), jnp.float32)
    state_out = normal_values(keys[6], (SEQUENCE_LENGTH, STATE), 1.0, 6.0, ((0, 16),), jnp.float32)
    skip_weight = jnp.clip(0.5 + 1.0 * jax.random.uniform(keys[7], (CHANNEL_SLICE,), jnp.float32) ** levels(keys[7], (CHANNEL_SLICE,), ((0, 16),), -0.2, 0.2), 0.5, 1.5)
    projection = normal_values(keys[8], (CHANNEL_SLICE, D), CHANNEL_SLICE ** -0.5, 0.0625, ((0, 16),))
    norm_gain = jnp.clip(1.0 + 0.18 * jax.random.normal(keys[9], (D,), jnp.float32), 0.1, 1.9)
    routes_keys = jax.random.split(jax.random.fold_in(keys[10], 1), SEQUENCE_LENGTH // CTX_TOK)
    routes_turns = jax.random.permutation(jax.random.fold_in(keys[10], 3), SEQUENCE_LENGTH // CTX_TOK)
    routes = jax.vmap(lambda own, number: routed_block(jax.random.fold_in(keys[10], 2), own, number, CTX_TOK, EXPERTS, 2, CAP, 2))(routes_keys, routes_turns).reshape((SEQUENCE_LENGTH, 2))
    route_weight = jnp.clip(0.2 + 0.8 * jax.random.uniform(keys[11], (SEQUENCE_LENGTH, 2), jnp.float32) ** levels(keys[11], (SEQUENCE_LENGTH, 2), ((0, 16),), -0.2, 0.2), 0.2, 1.0)
    up_weight = normal_values(keys[12], (EXPERTS, D, FF), D ** -0.5, 0.09375, ((0, 8), (2, 32)))
    down_weight = normal_values(keys[13], (EXPERTS, FF, D), FF ** -0.5, 0.0546875, ((0, 8), (1, 32)))
    return dict(residual=residual, mixer_input=mixer_input, mixer_gate=mixer_gate, step_size=step_size, decay_rate=decay_rate, state_in=state_in, state_out=state_out, skip_weight=skip_weight, projection=projection, norm_gain=norm_gain, routes=routes, route_weight=route_weight, up_weight=up_weight, down_weight=down_weight)


def mamba_scan(mixer_input, step_size, decay_rate, state_in, state_out, skip_weight):
    inputs = mixer_input.astype(jnp.float32)

    def advance(carry_state, pieces):
        input_row, step_row, in_row, out_row = pieces
        decays = jnp.exp(-step_row[None, :] * decay_rate)
        carry_state = decays * carry_state + (step_row * input_row)[None, :] * in_row[:, None]
        return (carry_state, lax.optimization_barrier(jnp.sum(out_row[:, None] * carry_state, axis=0)))
    initial = jnp.zeros(decay_rate.shape, jnp.float32)
    _, outputs = lax.scan(advance, initial, (inputs, step_size, state_in, state_out))
    return outputs + skip_weight[None, :] * inputs

def reference(residual, mixer_input, mixer_gate, step_size, decay_rate, state_in, state_out, skip_weight, projection, norm_gain, routes, route_weight, up_weight, down_weight):
    scanned = mamba_scan(mixer_input, step_size, decay_rate, state_in, state_out, skip_weight)
    gated_out = (scanned * jax.nn.silu(mixer_gate.astype(jnp.float32))).astype(jnp.bfloat16)
    updated = residual.astype(jnp.float32) + jnp.dot(gated_out, projection, preferred_element_type=jnp.float32)
    normed = (updated * lax.rsqrt(lax.optimization_barrier(jnp.mean(updated * updated, axis=1, keepdims=True)) + 1e-05) * norm_gain[None, :]).astype(jnp.bfloat16)
    groups = N_CTX * N_HALF
    group_width = FF // groups
    flat_routes = routes.reshape(N_CTX, CTX_TOK * 2)
    flat_weights = route_weight.reshape(N_CTX, CTX_TOK * 2)
    entries = jnp.arange(CTX_TOK * 2, dtype=jnp.int32)
    block_ids = jnp.arange(N_CTX, dtype=jnp.int32)
    token_ids = ((entries // 2)[None, :] + (block_ids * CTX_TOK)[:, None]).astype(jnp.int32)
    slot_total = N_CTX * CAP

    def one_expert(combined, expert_id):
        matches = flat_routes == expert_id
        slot_index = (jnp.cumsum(matches.astype(jnp.int32), axis=1) - 1).astype(jnp.int32)
        slot_place = jnp.where(matches, block_ids[:, None] * CAP + slot_index, slot_total).astype(jnp.int32).reshape(-1)
        slot_token = jnp.zeros((slot_total + 1,), jnp.int32).at[slot_place].set(token_ids.reshape(-1))[:slot_total]
        chosen = jnp.where(matches, flat_weights, jnp.zeros_like(flat_weights)).reshape(-1)
        slot_weight = jnp.zeros((slot_total + 1,), jnp.float32).at[slot_place].set(chosen)[:slot_total]
        gathered = normed[slot_token]
        hidden = jax.nn.silu(jnp.dot(gathered, up_weight[expert_id], preferred_element_type=jnp.float32)).astype(jnp.bfloat16)
        down_block = down_weight[expert_id]

        def add_group(accumulated, group_id):
            part_hidden = lax.dynamic_slice_in_dim(hidden, (group_id * group_width).astype(jnp.int32), group_width, 1)
            part_down = lax.dynamic_slice_in_dim(down_block, (group_id * group_width).astype(jnp.int32), group_width, 0)
            product = jnp.dot(part_hidden, part_down, preferred_element_type=jnp.float32).astype(jnp.bfloat16)
            product = lax.optimization_barrier(product)
            return (accumulated + product.astype(jnp.float32), None)
        expert_out, _ = lax.scan(add_group, jnp.zeros((slot_total, D), jnp.float32), jnp.arange(groups, dtype=jnp.int32))
        return (combined.at[slot_token].add(expert_out * slot_weight[:, None]), None)
    moe_out, _ = lax.scan(one_expert, jnp.zeros((N_CTX * CTX_TOK, D), jnp.float32), jnp.arange(EXPERTS, dtype=jnp.int32))
    return (updated + moe_out).astype(jnp.bfloat16)
```

```python
import functools

import jax
import jax.numpy as jnp
from jax import lax
from jax.experimental import pallas as pl
from jax.experimental.pallas import tpu as pltpu
from jax.sharding import PartitionSpec as P

F32 = jnp.float32
BF16 = jnp.bfloat16
TOK = 128
CH = 512
NS = 16
D = 4096
HD = 2048
FFL = 384
NZ = 8
NCTX = 16


def layer_kernel(
    residual,
    xin,
    gate,
    step,
    rate,
    sin,
    sout,
    skip,
    proj_hbm,
    gain,
    routes,
    rweight,
    up_hbm,
    down_hbm,
    out,
    proj,
    up,
    down,
    dec,
    drive,
    yacc,
    trans,
    carry,
    gsend,
    gmine,
    gpeer,
    psend,
    precv,
    own16,
    upd16,
    rows,
    chooser,
    selsend,
    selpeer,
    x,
    hid,
    part,
    r1,
    r2,
    r3,
    r4,
    qsend,
    q0,
    outs,
    csend,
    crecv,
    wsem,
    wsend,
    wrecv,
    carry_s,
    carry_r,
    one_s,
    one_r,
    zs1,
    zr1,
    zs2,
    zr2,
    zs3,
    zr3,
    ag_s,
    ag_r,
    s1,
    r1s,
    s2,
    r2s,
    s3,
    r3s,
    s4,
    r4s,
):
    c = lax.axis_index("ctx")
    z = lax.axis_index("exp")
    h = lax.axis_index("half")
    sending = []

    def send(src, dst, ssem, rsem, to):
        copy = pltpu.make_async_remote_copy(
            src_ref=src,
            dst_ref=dst,
            send_sem=ssem,
            recv_sem=rsem,
            device_id=to,
            device_id_type=pl.DeviceIdType.MESH,
        )
        copy.start()
        sending.append(copy)

    def arrived(dst, ssem, rsem):
        pltpu.make_async_remote_copy(
            src_ref=dst,
            dst_ref=dst,
            send_sem=ssem,
            recv_sem=rsem,
            device_id=sibling,
            device_id_type=pl.DeviceIdType.MESH,
        ).wait_recv()

    sibling = {"ctx": c, "exp": z, "half": 1 - h}

    def zpeer(d):
        return {"ctx": c, "exp": lax.rem(z + d, NZ), "half": h}

    cy, cx = lax.div(c, 4), lax.rem(c, 4)
    a = cx + h * (cy - cx)
    b = cy + h * (cx - cy)

    def ctx_at(da, db):
        return lax.rem(a + da, 4) * (1 + 3 * h) + lax.rem(b + db, 4) * (4 - 3 * h)

    def apeer(d):
        return {"ctx": ctx_at(d, 0), "exp": z, "half": h}

    def bpeer(d):
        return {"ctx": ctx_at(0, d), "exp": z, "half": h}

    local = [
        pltpu.make_async_copy(proj_hbm, proj.at[pl.ds(0, CH)], wsem.at[0]),
        pltpu.make_async_copy(up_hbm.at[0], up.at[:, pl.ds(0, FFL)], wsem.at[1]),
        pltpu.make_async_copy(down_hbm.at[0], down.at[pl.ds(0, FFL)], wsem.at[2]),
    ]
    for copy in local:
        copy.start()

    barrier = pltpu.get_barrier_semaphore()
    for d in range(1, NCTX):
        pl.semaphore_signal(
            barrier,
            inc=1,
            device_id={"ctx": lax.rem(c + d, NCTX), "exp": z, "half": h},
            device_id_type=pl.DeviceIdType.MESH,
        )
    for d in range(1, NZ):
        pl.semaphore_signal(
            barrier, inc=1, device_id=zpeer(d), device_id_type=pl.DeviceIdType.MESH
        )
    pl.semaphore_signal(
        barrier, inc=1, device_id=sibling, device_id_type=pl.DeviceIdType.MESH
    )
    pl.semaphore_wait(barrier, NCTX - 1 + NZ - 1 + 1)

    send(proj_hbm, proj.at[pl.ds(CH, CH)], wsend.at[0], wrecv.at[0], sibling)

    nrate = -rate[...]
    trans[...] = jnp.zeros_like(trans)
    trans[:, 0:NS] = sin[...]
    trans[:, NS : 2 * NS] = sout[...]
    trans[...] = trans[...].T
    drive[...] = step[...] * xin[...].astype(F32)

    def turned(first, base):
        return pltpu.roll(trans[first : first + NS, :], lax.rem(TOK - base, TOK), 1)

    def first_pass(tb, state):
        base = pl.multiple_of(tb * 8, 8)
        st8 = step[pl.ds(base, 8), :]
        dr8 = drive[pl.ds(base, 8), :]
        ins = turned(0, base)
        for i in range(8):
            decay = jnp.exp(st8[i : i + 1, :] * nrate)
            dec[base + i] = decay
            state = decay * state + dr8[i : i + 1, :] * ins[:, i : i + 1]
        return state

    zero_state = jnp.zeros((NS, CH), F32)
    carry[c, 0:NS, :] = lax.fori_loop(0, TOK // 8, first_pass, zero_state)
    carry[c, NS : NS + 8, :] = jnp.broadcast_to(
        jnp.sum(step[...], axis=0, keepdims=True), (8, CH)
    )

    for d in range(1, NCTX):

        @pl.when(c + d < NCTX)
        def _():
            pltpu.make_async_remote_copy(
                src_ref=carry.at[c],
                dst_ref=carry.at[c],
                send_sem=carry_s.at[d],
                recv_sem=carry_r.at[d],
                device_id={"ctx": c + d, "exp": z, "half": h},
                device_id_type=pl.DeviceIdType.MESH,
            ).start()

    send(up_hbm.at[0], up.at[:, pl.ds(FFL, FFL)], wsend.at[1], wrecv.at[1], sibling)
    send(down_hbm.at[0], down.at[pl.ds(FFL, FFL)], wsend.at[2], wrecv.at[2], sibling)

    hit0 = routes[:, 0:1] == z
    hit1 = routes[:, 1:2] == z
    hits = jnp.broadcast_to(jnp.where(hit0 | hit1, 1.0, 0.0).astype(F32), (TOK, TOK))
    weigh = jnp.where(hit0, rweight[:, 0:1], 0.0) + jnp.where(hit1, rweight[:, 1:2], 0.0)
    weigh = jnp.broadcast_to(weigh, (TOK, TOK))
    major = lax.broadcasted_iota(jnp.int32, (TOK, TOK), 0)
    minor = lax.broadcasted_iota(jnp.int32, (TOK, TOK), 1)
    token = 16 * ((z + (minor >> 4)) & 7) + 8 * h + (minor & 7)
    before = jnp.sum(jnp.where(major <= token, hits, 0.0), axis=0, keepdims=True)
    same = major == token
    named = jnp.sum(jnp.where(same, hits, 0.0), axis=0, keepdims=True)
    weight_row = jnp.sum(jnp.where(same, weigh, 0.0), axis=0, keepdims=True)
    who = major >> 6
    slot = 32 * (h + who * (1 - 2 * h)) + (major & 31)
    chosen = jnp.where(
        (((major >> 5) & 1) == ((minor >> 3) & 1)) & (before == (slot + 1).astype(F32)),
        named,
        0.0,
    )
    chooser[...] = chosen.astype(BF16)
    weight_col = jnp.broadcast_to(weight_row, (TOK, TOK)).T[:, 0:1]

    for d in range(1, NCTX):

        @pl.when(c >= d)
        def _():
            arrived(carry.at[c - d], carry_s.at[d], carry_r.at[d])

    def enter(j, state):
        return jnp.exp(carry[j, NS : NS + 1, :] * nrate) * state + carry[j, 0:NS, :]

    entering = lax.fori_loop(0, c, enter, zero_state)

    def second_pass(tb, state):
        base = pl.multiple_of(tb * 8, 8)
        dr8 = drive[pl.ds(base, 8), :]
        ins = turned(0, base)
        outw = turned(NS, base)
        for i in range(8):
            state = dec[base + i] * state + dr8[i : i + 1, :] * ins[:, i : i + 1]
            yacc[pl.ds(base + i, 1), :] = jnp.sum(
                state * outw[:, i : i + 1], axis=0, keepdims=True
            )
        return state

    lax.fori_loop(0, TOK // 8, second_pass, entering)

    gates = gate[...].astype(F32)
    yacc[...] = (yacc[...] + skip[...] * xin[...].astype(F32)) * (
        gates / (1.0 + jnp.exp(-gates))
    )

    def eights(whose):
        return jnp.concatenate(
            [
                yacc[pl.ds(pl.multiple_of(16 * lax.rem(z + d, NZ) + 8 * whose, 8), 8), :]
                for d in range(NZ)
            ],
            axis=0,
        ).astype(BF16)

    gsend[...] = eights(1 - h)
    send(gsend, gpeer, one_s.at[0], one_r.at[0], sibling)
    gmine[...] = eights(h)

    local[0].wait()
    arrived(proj.at[pl.ds(CH, CH)], wsend.at[0], wrecv.at[0])
    arrived(gpeer, one_s.at[0], one_r.at[0])

    def project(n, _):
        def block(first):
            cols = pl.ds(pl.multiple_of(first + n * 512, 512), 512)
            return jnp.dot(
                gmine[...], proj[0:CH, cols], preferred_element_type=F32
            ) + jnp.dot(gpeer[...], proj[CH : 2 * CH, cols], preferred_element_type=F32)

        both = jnp.concatenate(
            [block(0).reshape(NZ, 8, 512), block(HD).reshape(NZ, 8, 512)], axis=1
        )
        cols = pl.ds(pl.multiple_of(n * 512, 512), 512)
        own16[:, cols] = both[0]
        psend[:, :, cols] = both.astype(BF16)
        return 0

    lax.fori_loop(0, HD // 512, project, 0)
    order = (4, 3, 5, 2, 6, 1, 7)
    for d in order:
        send(psend.at[d], precv.at[d], zs1.at[d], zr1.at[d], zpeer(d))

    res = residual[...].astype(F32)
    total = own16[...] + jnp.concatenate([res[:, :HD], res[:, HD:]], axis=0)
    for d in reversed(order):
        arrived(precv.at[d], zs1.at[d], zr1.at[d])
        total = total + precv[d].astype(F32)
    upd16[...] = total
    squares = jnp.sum(total * total, axis=1, keepdims=True)
    scale = lax.rsqrt((squares[0:8] + squares[8:16]) * (1.0 / D) + 1e-05)
    gains = jnp.concatenate(
        [
            jnp.broadcast_to(gain[:, :HD], (8, HD)),
            jnp.broadcast_to(gain[:, HD:], (8, HD)),
        ],
        axis=0,
    )
    rows[0] = (total * jnp.concatenate([scale, scale], axis=0) * gains).astype(BF16)
    for d in order:
        send(rows.at[0], rows.at[NZ - d], zs2.at[d], zr2.at[d], zpeer(d))
    for d in reversed(order):
        arrived(rows.at[NZ - d], zs2.at[d], zr2.at[d])

    def select(n, _):
        cols = pl.ds(pl.multiple_of(n * 512, 512), 512)
        picked = jnp.dot(
            chooser[...], rows[:, :, cols].reshape(TOK, 512), preferred_element_type=F32
        ).astype(BF16)
        selsend[:, :, cols] = picked[64:128].reshape(2, 32, 512)
        x[0, 0, :, :, cols] = picked[0:64].reshape(2, 32, 512)
        return 0

    lax.fori_loop(0, HD // 512, select, 0)
    send(selsend, selpeer, one_s.at[1], one_r.at[1], sibling)
    arrived(selpeer, one_s.at[1], one_r.at[1])
    x[0, 0] = (x[0, 0].astype(F32) + selpeer[...].astype(F32)).astype(BF16)

    tag = [0]

    def gather(rb, ra, f, to, lb, la):
        send(
            x.at[rb, ra, f], x.at[lb, la, f], ag_s.at[tag[0]], ag_r.at[lb, la, f], to
        )
        tag[0] += 1

    def have(rb, ra, f):
        arrived(x.at[rb, ra, f], ag_s.at[0], ag_r.at[rb, ra, f])

    def along_b(ra, f):
        gather(0, ra, f, bpeer(1), 3, ra)
        gather(0, ra, f, bpeer(3), 1, ra)

    for f in range(2):
        gather(0, 0, f, apeer(1), 0, 3)
        gather(0, 0, f, apeer(3), 0, 1)
    for f in range(2):
        along_b(0, f)
    for f in range(2):
        have(0, 3, f)
        if f == 0:
            gather(0, 3, 0, apeer(1), 0, 2)
        have(0, 1, f)
        if f == 1:
            gather(0, 1, 1, apeer(3), 0, 2)
        along_b(3, f)
        along_b(1, f)

    def pass_on(ra):
        for f in range(2):
            have(3, ra, f)
            if f == 0:
                gather(3, ra, 0, bpeer(1), 2, ra)
            have(1, ra, f)
            if f == 1:
                gather(1, ra, 1, bpeer(3), 2, ra)

    for f in range(2):
        have(0, 2, f)
        along_b(2, f)
    pass_on(0)

    local[1].wait()
    local[2].wait()
    arrived(up.at[:, pl.ds(FFL, FFL)], wsend.at[1], wrecv.at[1])
    arrived(down.at[pl.ds(FFL, FFL)], wsend.at[2], wrecv.at[2])

    def experts(rb):
        def widen(n, _):
            cols = pl.ds(pl.multiple_of(n * 256, 256), 256)
            pre = jnp.dot(
                x[rb, :, 0].reshape(TOK, HD), up[0:HD, cols], preferred_element_type=F32
            ) + jnp.dot(
                x[rb, :, 1].reshape(TOK, HD), up[HD:D, cols], preferred_element_type=F32
            )
            hid[:, cols] = (pre / (1.0 + jnp.exp(-pre))).astype(BF16)
            return 0

        lax.fori_loop(0, 2 * FFL // 256, widen, 0)

        def narrow(n, _):
            cols = pl.ds(pl.multiple_of(n * 256, 256), 256)
            for f in range(2):
                wide = pl.ds(pl.multiple_of(f * HD + n * 256, 256), 256)
                part[rb, :, f, :, cols] = (
                    jnp.dot(hid[...], down[:, wide], preferred_element_type=F32)
                    .astype(BF16)
                    .reshape(4, 32, 256)
                )
            return 0

        lax.fori_loop(0, HD // 256, narrow, 0)

    experts(0)
    for ra in (3, 1, 2):
        pass_on(ra)
    experts(1)
    experts(3)

    turns = (2, 1, 3, 0)
    for ra in turns:
        send(part.at[1, ra, 1], r2.at[0, ra, 1], s2.at[0, ra, 1], r2s.at[0, ra, 1], bpeer(1))
        send(part.at[3, ra, 0], r2.at[1, ra, 0], s2.at[1, ra, 0], r2s.at[1, ra, 0], bpeer(3))
    for ra in range(4):
        for f in range(2):
            have(2, ra, f)
    experts(2)
    for ra in turns:
        send(part.at[2, ra, 0], r1.at[0, ra], s1.at[0, ra], r1s.at[0, ra], bpeer(1))
        send(part.at[2, ra, 1], r1.at[1, ra], s1.at[1, ra], r1s.at[1, ra], bpeer(3))
    for ra in turns:
        arrived(r1.at[0, ra], s1.at[0, ra], r1s.at[0, ra])
        part[1, ra, 0] = (part[1, ra, 0].astype(F32) + r1[0, ra].astype(F32)).astype(BF16)
        send(part.at[1, ra, 0], r2.at[0, ra, 0], s2.at[0, ra, 0], r2s.at[0, ra, 0], bpeer(1))
        arrived(r1.at[1, ra], s1.at[1, ra], r1s.at[1, ra])
        part[3, ra, 1] = (part[3, ra, 1].astype(F32) + r1[1, ra].astype(F32)).astype(BF16)
        send(part.at[3, ra, 1], r2.at[1, ra, 1], s2.at[1, ra, 1], r2s.at[1, ra, 1], bpeer(3))

    def along_b_sum(ra, f):
        for side in range(2):
            arrived(r2.at[side, ra, f], s2.at[side, ra, f], r2s.at[side, ra, f])
        return part[0, ra, f].astype(F32) + r2[0, ra, f].astype(F32) + r2[1, ra, f].astype(F32)

    for f in range(2):
        qsend[2, f] = along_b_sum(2, f).astype(BF16)
        send(
            qsend.at[2, f], r3.at[f], s3.at[f], r3s.at[f], apeer(1) if f == 0 else apeer(3)
        )
    for ra, early in ((1, 1), (3, 0)):
        side = 0 if ra == 1 else 1
        qsend[ra, early] = along_b_sum(ra, early).astype(BF16)
        send(
            qsend.at[ra, early],
            r4.at[side, early],
            s4.at[side, early],
            r4s.at[side, early],
            apeer(ra),
        )
    for ra, late in ((1, 0), (3, 1)):
        side = 0 if ra == 1 else 1
        summed = along_b_sum(ra, late)
        arrived(r3.at[late], s3.at[late], r3s.at[late])
        qsend[ra, late] = (summed + r3[late].astype(F32)).astype(BF16)
        send(
            qsend.at[ra, late],
            r4.at[side, late],
            s4.at[side, late],
            r4s.at[side, late],
            apeer(ra),
        )
    for f in range(2):
        q0[f] = along_b_sum(0, f)
    for f in (1, 0):
        for side in range(2):
            arrived(r4.at[side, f], s4.at[side, f], r4s.at[side, f])
        outs[0, f] = (q0[f] + r4[0, f].astype(F32) + r4[1, f].astype(F32)).astype(BF16)

    send(outs.at[0], outs.at[1], one_s.at[2], one_r.at[2], sibling)
    arrived(outs.at[1], one_s.at[2], one_r.at[2])

    def spread(n, _):
        cols = pl.ds(pl.multiple_of(n * 512, 512), 512)
        given = (
            lax.dot_general(
                chooser[...],
                outs[:, :, :, cols].reshape(TOK, 512),
                (((0,), (0,)), ((), ())),
                preferred_element_type=F32,
            )
            * weight_col
        ).reshape(NZ, 16, 512)
        own16[:, cols] = given[0]
        csend[:, :, cols] = given.astype(BF16)
        return 0

    lax.fori_loop(0, HD // 512, spread, 0)
    for d in order:
        send(csend.at[d], crecv.at[d], zs3.at[d], zr3.at[d], zpeer(d))
    total = upd16[...] + own16[...]
    for d in reversed(order):
        arrived(crecv.at[d], zs3.at[d], zr3.at[d])
        total = total + crecv[d].astype(F32)
    out[:, 0:HD] = total[0:8].astype(BF16)
    out[:, HD:D] = total[8:16].astype(BF16)

    for copy in sending:
        copy.wait_send()
    for d in range(1, NCTX):

        @pl.when(c + d < NCTX)
        def _():
            pltpu.make_async_remote_copy(
                src_ref=carry.at[c],
                dst_ref=carry.at[c],
                send_sem=carry_s.at[d],
                recv_sem=carry_r.at[d],
                device_id=sibling,
                device_id_type=pl.DeviceIdType.MESH,
            ).wait_send()


def per_device(
    residual,
    mixer_input,
    mixer_gate,
    step_size,
    decay_rate,
    state_in,
    state_out,
    skip_weight,
    projection,
    norm_gain,
    routes,
    route_weight,
    up_weight,
    down_weight,
):
    vmem = pl.BlockSpec(memory_space=pltpu.VMEM)
    hbm = pl.BlockSpec(memory_space=pl.ANY)
    dma = pltpu.SemaphoreType.DMA
    scratch = [
        pltpu.VMEM((2 * CH, D), BF16),
        pltpu.VMEM((D, 2 * FFL), BF16),
        pltpu.VMEM((2 * FFL, D), BF16),
        pltpu.VMEM((TOK, NS, CH), F32),
        pltpu.VMEM((TOK, CH), F32),
        pltpu.VMEM((TOK, CH), F32),
        pltpu.VMEM((TOK, TOK), F32),
        pltpu.VMEM((NCTX, NS + 8, CH), F32),
        pltpu.VMEM((64, CH), BF16),
        pltpu.VMEM((64, CH), BF16),
        pltpu.VMEM((64, CH), BF16),
        pltpu.VMEM((NZ, 16, HD), BF16),
        pltpu.VMEM((NZ, 16, HD), BF16),
        pltpu.VMEM((16, HD), F32),
        pltpu.VMEM((16, HD), F32),
        pltpu.VMEM((NZ, 16, HD), BF16),
        pltpu.VMEM((TOK, TOK), BF16),
        pltpu.VMEM((2, 32, HD), BF16),
        pltpu.VMEM((2, 32, HD), BF16),
        pltpu.VMEM((4, 4, 2, 32, HD), BF16),
        pltpu.VMEM((TOK, 2 * FFL), BF16),
        pltpu.VMEM((4, 4, 2, 32, HD), BF16),
        pltpu.VMEM((2, 4, 32, HD), BF16),
        pltpu.VMEM((2, 4, 2, 32, HD), BF16),
        pltpu.VMEM((2, 32, HD), BF16),
        pltpu.VMEM((2, 2, 32, HD), BF16),
        pltpu.VMEM((4, 2, 32, HD), BF16),
        pltpu.VMEM((2, 32, HD), F32),
        pltpu.VMEM((2, 2, 32, HD), BF16),
        pltpu.VMEM((NZ, 16, HD), BF16),
        pltpu.VMEM((NZ, 16, HD), BF16),
        dma((3,)),
        dma((3,)),
        dma((3,)),
        dma((NCTX,)),
        dma((NCTX,)),
        dma((3,)),
        dma((3,)),
        dma((NZ,)),
        dma((NZ,)),
        dma((NZ,)),
        dma((NZ,)),
        dma((NZ,)),
        dma((NZ,)),
        dma((40,)),
        dma((4, 4, 2)),
        dma((2, 4)),
        dma((2, 4)),
        dma((2, 4, 2)),
        dma((2, 4, 2)),
        dma((2,)),
        dma((2,)),
        dma((2, 2)),
        dma((2, 2)),
    ]
    return pl.pallas_call(
        layer_kernel,
        out_shape=jax.ShapeDtypeStruct(residual.shape, BF16),
        in_specs=[
            vmem, vmem, vmem, vmem, vmem, vmem, vmem, vmem,
            hbm, vmem, vmem, vmem, hbm, hbm,
        ],
        out_specs=vmem,
        scratch_shapes=scratch,
        compiler_params=pltpu.CompilerParams(
            collective_id=0, has_side_effects=True, vmem_limit_bytes=58 * 1024 * 1024
        ),
    )(
        residual,
        mixer_input,
        mixer_gate,
        step_size,
        decay_rate,
        state_in,
        state_out,
        skip_weight.reshape(1, CH),
        projection,
        norm_gain.reshape(1, D),
        routes,
        route_weight,
        up_weight,
        down_weight,
    )


def solution(mesh):
    in_specs = (
        P(("ctx", "exp", "half"), None),
        P("ctx", ("exp", "half")),
        P("ctx", ("exp", "half")),
        P("ctx", ("exp", "half")),
        P(None, ("exp", "half")),
        P("ctx", None),
        P("ctx", None),
        P(("exp", "half")),
        P(("exp", "half"), None),
        P(),
        P("ctx", None),
        P("ctx", None),
        P("exp", None, ("ctx", "half")),
        P("exp", ("ctx", "half"), None),
    )
    out_specs = P(("ctx", "exp", "half"), None)
    return jax.shard_map(
        per_device, mesh=mesh, in_specs=in_specs, out_specs=out_specs, check_vma=False
    )
```

```python
import jax
import jax.numpy as jnp
from jax import lax
from jax.experimental import pallas as pl
from jax.experimental.pallas import tpu as pltpu
from jax.sharding import PartitionSpec as P

F32 = jnp.float32
BF16 = jnp.bfloat16
TOK = 128
CH = 512
NS = 16
D = 4096
FFL = 384
NZ = 8
NCTX = 16
NG = 4
W = 512


def layer_kernel(
    residual_hbm,
    xin_hbm,
    gate_hbm,
    step_hbm,
    rate_hbm,
    sin_hbm,
    sout_hbm,
    skip,
    proj_hbm,
    gain,
    routes,
    rweight,
    up_hbm,
    down_hbm,
    out,
    residual,
    xin,
    gate,
    step,
    rate,
    sin,
    sout,
    proj,
    up,
    down,
    dec,
    drive,
    yacc,
    carry,
    sums,
    gsend,
    gmine,
    gpeer,
    psend,
    rp0,
    rp,
    own16,
    upd16,
    rows,
    chooser,
    selsend,
    selpeer,
    x,
    hid,
    part,
    r1,
    r2,
    r3,
    r4,
    qsend,
    outs,
    csend,
    crecv,
    isem,
    wsem,
    wsend,
    wrecv,
    carry_s,
    carry_r,
    sum_s,
    sum_r,
    gate_s,
    gate_r,
    sel_s,
    sel_r,
    out_s,
    out_r,
    p0_s,
    p0_r,
    p_s,
    p_r,
    zs2,
    zr2,
    zs3,
    zr3,
    ag_s,
    ag_r,
    s1,
    r1s,
    s2,
    r2s,
    s3,
    r3s,
    s4,
    r4s,
):
    c = lax.axis_index("ctx")
    z = lax.axis_index("exp")
    h = lax.axis_index("half")
    sending = []

    def remote(src, dst, ssem, rsem, to):
        return pltpu.make_async_remote_copy(
            src_ref=src,
            dst_ref=dst,
            send_sem=ssem,
            recv_sem=rsem,
            device_id=to,
            device_id_type=pl.DeviceIdType.MESH,
        )

    def send(src, dst, ssem, rsem, to):
        copy = remote(src, dst, ssem, rsem, to)
        copy.start()
        sending.append(copy)

    sibling = {"ctx": c, "exp": z, "half": 1 - h}

    def arrived(dst, ssem, rsem):
        remote(dst, dst, ssem, rsem, sibling).wait_recv()

    def zpeer(d):
        return {"ctx": c, "exp": lax.rem(z + d, NZ), "half": h}

    cy, cx = lax.div(c, 4), lax.rem(c, 4)
    a = cx + h * (cy - cx)
    b = cy + h * (cx - cy)

    def ctx_at(da, db):
        return lax.rem(a + da, 4) * (1 + 3 * h) + lax.rem(b + db, 4) * (4 - 3 * h)

    def apeer(d):
        return {"ctx": ctx_at(d, 0), "exp": z, "half": h}

    def bpeer(d):
        return {"ctx": ctx_at(0, d), "exp": z, "half": h}

    inputs = [
        pltpu.make_async_copy(src, dst, isem.at[i])
        for i, (src, dst) in enumerate(
            (
                (step_hbm, step),
                (xin_hbm, xin),
                (rate_hbm, rate),
                (sin_hbm, sin),
                (sout_hbm, sout),
                (gate_hbm, gate),
                (residual_hbm, residual),
            )
        )
    ]
    local = [
        pltpu.make_async_copy(proj_hbm, proj.at[pl.ds(0, CH)], wsem.at[0]),
        pltpu.make_async_copy(up_hbm.at[0], up.at[:, pl.ds(0, FFL)], wsem.at[1]),
        pltpu.make_async_copy(down_hbm.at[0], down.at[pl.ds(0, FFL)], wsem.at[2]),
    ]
    for copy in inputs + local:
        copy.start()

    barrier = pltpu.get_barrier_semaphore()
    for d in range(1, NCTX):
        pl.semaphore_signal(
            barrier,
            inc=1,
            device_id={"ctx": lax.rem(c + d, NCTX), "exp": z, "half": h},
            device_id_type=pl.DeviceIdType.MESH,
        )
    for d in range(1, NZ):
        pl.semaphore_signal(
            barrier, inc=1, device_id=zpeer(d), device_id_type=pl.DeviceIdType.MESH
        )
    pl.semaphore_signal(
        barrier, inc=1, device_id=sibling, device_id_type=pl.DeviceIdType.MESH
    )

    for copy in inputs:
        copy.wait()
    nrate = -rate[...]
    drive[...] = step[...] * xin[...].astype(F32)
    sums[c] = jnp.sum(step[...], axis=0, keepdims=True)

    def turned(ref, base):
        return pltpu.roll(ref[...], lax.rem(TOK - base, TOK), 1)

    def first_pass(tb, state):
        base = pl.multiple_of(tb * 8, 8)
        st8 = step[pl.ds(base, 8), :]
        dr8 = drive[pl.ds(base, 8), :]
        ins = turned(sin, base)
        for i in range(8):
            decay = jnp.exp(st8[i : i + 1, :] * nrate)
            dec[base + i] = decay
            state = decay * state + dr8[i : i + 1, :] * ins[:, i : i + 1]
        return state

    zero_state = jnp.zeros((NS, CH), F32)
    carry[c] = lax.fori_loop(0, TOK // 8, first_pass, zero_state).astype(BF16)

    pl.semaphore_wait(barrier, NCTX - 1 + NZ - 1 + 1)

    def later(d):
        return {"ctx": c + d, "exp": z, "half": h}

    for d in range(1, NCTX):

        @pl.when(c + d < NCTX)
        def _():
            remote(carry.at[c], carry.at[c], carry_s.at[d], carry_r.at[d], later(d)).start()
            remote(sums.at[c], sums.at[c], sum_s.at[d], sum_r.at[d], later(d)).start()

    send(proj_hbm, proj.at[pl.ds(CH, CH)], wsend.at[0], wrecv.at[0], sibling)
    send(up_hbm.at[0], up.at[:, pl.ds(FFL, FFL)], wsend.at[1], wrecv.at[1], sibling)
    send(down_hbm.at[0], down.at[pl.ds(FFL, FFL)], wsend.at[2], wrecv.at[2], sibling)

    hit0 = routes[0:1, :] == z
    hit1 = routes[1:2, :] == z
    hits = jnp.where(hit0 | hit1, 1.0, 0.0).astype(F32)
    weigh = jnp.where(hit0, rweight[0:1, :], 0.0) + jnp.where(hit1, rweight[1:2, :], 0.0)
    hits = jnp.broadcast_to(hits, (TOK, TOK)).T
    weigh = jnp.broadcast_to(weigh, (TOK, TOK)).T
    major = lax.broadcasted_iota(jnp.int32, (TOK, TOK), 0)
    minor = lax.broadcasted_iota(jnp.int32, (TOK, TOK), 1)
    token = 16 * ((z + (minor >> 4)) & 7) + 8 * h + (minor & 7)
    before = jnp.sum(jnp.where(major <= token, hits, 0.0), axis=0, keepdims=True)
    same = major == token
    named = jnp.sum(jnp.where(same, hits, 0.0), axis=0, keepdims=True)
    weight_row = jnp.sum(jnp.where(same, weigh, 0.0), axis=0, keepdims=True)
    who = major >> 6
    slot = 32 * (h + who * (1 - 2 * h)) + (major & 31)
    chosen = jnp.where(
        (((major >> 5) & 1) == ((minor >> 3) & 1)) & (before == (slot + 1).astype(F32)),
        named,
        0.0,
    )
    chooser[...] = chosen.astype(BF16)
    weight_col = jnp.broadcast_to(weight_row, (TOK, TOK)).T[:, 0:1]

    for d in range(1, NCTX):

        @pl.when(c >= d)
        def _():
            arrived(carry.at[c - d], carry_s.at[d], carry_r.at[d])
            arrived(sums.at[c - d], sum_s.at[d], sum_r.at[d])

    def enter(j, state):
        return jnp.exp(sums[j] * nrate) * state + carry[j].astype(F32)

    entering = lax.fori_loop(0, c, enter, zero_state)

    def second_pass(tb, state):
        base = pl.multiple_of(tb * 8, 8)
        dr8 = drive[pl.ds(base, 8), :]
        ins = turned(sin, base)
        outw = turned(sout, base)
        for i in range(8):
            state = dec[base + i] * state + dr8[i : i + 1, :] * ins[:, i : i + 1]
            yacc[pl.ds(base + i, 1), :] = jnp.sum(
                state * outw[:, i : i + 1], axis=0, keepdims=True
            )
        return state

    lax.fori_loop(0, TOK // 8, second_pass, entering)

    gates = gate[...].astype(F32)
    yacc[...] = (yacc[...] + skip[...] * xin[...].astype(F32)) * (
        gates / (1.0 + jnp.exp(-gates))
    )

    def eights(whose):
        return jnp.concatenate(
            [
                yacc[pl.ds(pl.multiple_of(16 * lax.rem(z + d, NZ) + 8 * whose, 8), 8), :]
                for d in range(NZ)
            ],
            axis=0,
        ).astype(BF16)

    gsend[...] = eights(1 - h)
    send(gsend, gpeer, gate_s.at[0], gate_r.at[0], sibling)
    gmine[...] = eights(h)

    local[0].wait()
    arrived(proj.at[pl.ds(CH, CH)], wsend.at[0], wrecv.at[0])
    arrived(gpeer, gate_s.at[0], gate_r.at[0])

    def project(g, _):
        def block(f):
            cols = pl.ds(pl.multiple_of((2 * g + f) * W, W), W)
            return (
                jnp.dot(gmine[...], proj[0:CH, cols], preferred_element_type=F32)
                + jnp.dot(gpeer[...], proj[CH : 2 * CH, cols], preferred_element_type=F32)
            ).reshape(NZ, 8, W)

        both = jnp.concatenate([block(0), block(1)], axis=1)
        own16[g] = both[0]
        psend[:, g] = both.astype(BF16)
        return 0

    lax.fori_loop(0, NG, project, 0)

    def ring(way, pos, half, slot):
        send(
            psend.at[pos, pl.ds(2 * half, 2)],
            rp.at[way, slot, half],
            p_s.at[way, slot, half],
            p_r.at[way, slot, half],
            zpeer(1) if way == 0 else zpeer(NZ - 1),
        )

    def add_in(pos, half, got):
        mine = psend[pos, 2 * half : 2 * half + 2].astype(F32)
        psend[pos, 2 * half : 2 * half + 2] = (mine + got.astype(F32)).astype(BF16)

    for way in range(2):
        send(
            psend.at[4, pl.ds(2 * way, 2)],
            rp0.at[way],
            p0_s.at[way],
            p0_r.at[way],
            zpeer(1) if way == 0 else zpeer(NZ - 1),
        )
    for way in range(2):
        ring(way, 3 if way == 0 else 5, 1 - way, 0)
    for way in range(2):
        arrived(rp0.at[way], p0_s.at[way], p0_r.at[way])
        pos = 3 if way == 0 else 5
        add_in(pos, way, rp0[way])
        ring(way, pos, way, 0)
    for slot in range(2):
        for turn in range(2):
            for way in range(2):
                half = 1 - way if turn == 0 else way
                arrived(rp.at[way, slot, half], p_s.at[way, slot, half], p_r.at[way, slot, half])
                pos = 2 - slot if way == 0 else 6 + slot
                add_in(pos, half, rp[way, slot, half])
                ring(way, pos, half, slot + 1)
    squares = jnp.zeros((16, 1), F32)
    for half in range(2):
        for way in range(2):
            arrived(rp.at[way, 2, half], p_s.at[way, 2, half], p_r.at[way, 2, half])
    for g in range(NG):
        res = residual[:, 2 * W * g : 2 * W * (g + 1)].astype(F32)
        total = own16[g] + jnp.concatenate([res[:, :W], res[:, W:]], axis=0)
        for way in range(2):
            total = total + rp[way, 2, g // 2, g % 2].astype(F32)
        upd16[g] = total
        squares = squares + jnp.sum(total * total, axis=1, keepdims=True)

    scale = lax.rsqrt((squares[0:8] + squares[8:16]) * (1.0 / D) + 1e-05)
    scale = jnp.concatenate([scale, scale], axis=0)
    order = (4, 3, 5, 2, 6, 1, 7)
    for g in range(NG):
        gains = jnp.concatenate(
            [
                jnp.broadcast_to(gain[:, (2 * g + f) * W : (2 * g + f + 1) * W], (8, W))
                for f in range(2)
            ],
            axis=0,
        )
        rows[g, 0] = (upd16[g] * scale * gains).astype(BF16)
        for d in order:
            send(rows.at[g, 0], rows.at[g, NZ - d], zs2.at[g, d], zr2.at[g, d], zpeer(d))

    def select(g):
        for d in reversed(order):
            arrived(rows.at[g, NZ - d], zs2.at[g, d], zr2.at[g, d])
        picked = jnp.dot(
            chooser[...], rows[g].reshape(TOK, W), preferred_element_type=F32
        )
        selsend[g] = picked[64:128].astype(BF16).reshape(2, 32, W)
        send(selsend.at[g], selpeer.at[g], sel_s.at[g], sel_r.at[g], sibling)
        arrived(selpeer.at[g], sel_s.at[g], sel_r.at[g])
        x[0, 0, 2 * g : 2 * g + 2] = (
            picked[0:64].reshape(2, 32, W) + selpeer[g].astype(F32)
        ).astype(BF16)

    tag = [0]

    def gather(rb, ra, e, to, lb, la):
        send(x.at[rb, ra, e], x.at[lb, la, e], ag_s.at[tag[0]], ag_r.at[lb, la, e], to)
        tag[0] += 1

    def have(rb, ra, e):
        arrived(x.at[rb, ra, e], ag_s.at[0], ag_r.at[rb, ra, e])

    def along_b(ra, e):
        gather(0, ra, e, bpeer(1), 3, ra)
        gather(0, ra, e, bpeer(3), 1, ra)

    def begin(g):
        for e in (2 * g, 2 * g + 1):
            gather(0, 0, e, apeer(1), 0, 3)
            gather(0, 0, e, apeer(3), 0, 1)
        for e in (2 * g, 2 * g + 1):
            along_b(0, e)

    def neighbours(g):
        for e in (2 * g, 2 * g + 1):
            have(0, 3, e)
            if e % 2 == 0:
                gather(0, 3, e, apeer(1), 0, 2)
            have(0, 1, e)
            if e % 2 == 1:
                gather(0, 1, e, apeer(3), 0, 2)
            along_b(3, e)
            along_b(1, e)

    def opposite(g):
        for e in (2 * g, 2 * g + 1):
            have(0, 2, e)
            along_b(2, e)

    def pass_on(g, ra):
        for e in (2 * g, 2 * g + 1):
            have(3, ra, e)
            if e % 2 == 0:
                gather(3, ra, e, bpeer(1), 2, ra)
            have(1, ra, e)
            if e % 2 == 1:
                gather(1, ra, e, bpeer(3), 2, ra)

    for turn in range(NG + 3):
        if turn < NG:
            select(turn)
            begin(turn)
        if 0 <= turn - 1 < NG:
            neighbours(turn - 1)
        if 0 <= turn - 2 < NG:
            opposite(turn - 2)
            pass_on(turn - 2, 0)
        if 0 <= turn - 3 < NG:
            pass_on(turn - 3, 3)
            pass_on(turn - 3, 1)

    local[1].wait()
    local[2].wait()
    arrived(up.at[:, pl.ds(FFL, FFL)], wsend.at[1], wrecv.at[1])
    arrived(down.at[pl.ds(FFL, FFL)], wsend.at[2], wrecv.at[2])

    def widen(rb):
        def body(n, _):
            cols = pl.ds(pl.multiple_of(n * 256, 256), 256)
            pre = jnp.zeros((TOK, 256), F32)
            for e in range(2 * NG):
                pre = pre + jnp.dot(
                    x[rb, :, e].reshape(TOK, W),
                    up[e * W : (e + 1) * W, cols],
                    preferred_element_type=F32,
                )
            hid[:, cols] = (pre / (1.0 + jnp.exp(-pre))).astype(BF16)
            return 0

        lax.fori_loop(0, 2 * FFL // 256, body, 0)

    def narrow(rb, g):
        for e in (2 * g, 2 * g + 1):
            part[rb, :, e] = (
                jnp.dot(hid[...], down[:, e * W : (e + 1) * W], preferred_element_type=F32)
                .astype(BF16)
                .reshape(4, 32, W)
            )

    turns = (2, 1, 3, 0)

    def sum_b(side, ra, e):
        send(
            part.at[1 + 2 * side, ra, e],
            r2.at[side, ra, e],
            s2.at[side, ra, e],
            r2s.at[side, ra, e],
            bpeer(1 + 2 * side),
        )

    widen(0)
    for g in range(NG):
        narrow(0, g)
    for g in range(NG):
        pass_on(g, 2)
    for side in range(2):
        widen(1 + 2 * side)
        for g in range(NG):
            narrow(1 + 2 * side, g)
            for ra in turns:
                sum_b(side, ra, 2 * g + 1 - side)
    for ra in range(4):
        for e in range(2 * NG):
            have(2, ra, e)
    widen(2)
    for g in range(NG):
        narrow(2, g)
        for ra in turns:
            for side in range(2):
                send(
                    part.at[2, ra, 2 * g + side],
                    r1.at[side, ra, g],
                    s1.at[side, ra, g],
                    r1s.at[side, ra, g],
                    bpeer(1 + 2 * side),
                )

    def add_b(g):
        for ra in turns:
            for side in range(2):
                e = 2 * g + side
                arrived(r1.at[side, ra, g], s1.at[side, ra, g], r1s.at[side, ra, g])
                part[1 + 2 * side, ra, e] = (
                    part[1 + 2 * side, ra, e].astype(F32) + r1[side, ra, g].astype(F32)
                ).astype(BF16)
                sum_b(side, ra, e)

    def summed_b(ra, e):
        for side in range(2):
            arrived(r2.at[side, ra, e], s2.at[side, ra, e], r2s.at[side, ra, e])
        return part[0, ra, e].astype(F32) + r2[0, ra, e].astype(F32) + r2[1, ra, e].astype(F32)

    def sum_a(side, e):
        send(
            qsend.at[1 + 2 * side, e],
            r4.at[side, e],
            s4.at[side, e],
            r4s.at[side, e],
            apeer(1 + 2 * side),
        )

    def start_a(g):
        for side in range(2):
            e = 2 * g + side
            qsend[2, e] = summed_b(2, e).astype(BF16)
            send(qsend.at[2, e], r3.at[e], s3.at[e], r3s.at[e], apeer(1 + 2 * side))
        for side in range(2):
            e = 2 * g + 1 - side
            qsend[1 + 2 * side, e] = summed_b(1 + 2 * side, e).astype(BF16)
            sum_a(side, e)

    def add_a(g):
        for side in range(2):
            e = 2 * g + side
            total = summed_b(1 + 2 * side, e)
            arrived(r3.at[e], s3.at[e], r3s.at[e])
            qsend[1 + 2 * side, e] = (total + r3[e].astype(F32)).astype(BF16)
            sum_a(side, e)

    def finish_a(g):
        for f in range(2):
            e = 2 * g + f
            total = summed_b(0, e)
            for side in range(2):
                arrived(r4.at[side, e], s4.at[side, e], r4s.at[side, e])
                total = total + r4[side, e].astype(F32)
            outs[g, 0, f] = total.astype(BF16)
        send(outs.at[g, 0], outs.at[g, 1], out_s.at[g], out_r.at[g], sibling)

    def spread(g):
        arrived(outs.at[g, 1], out_s.at[g], out_r.at[g])
        given = (
            lax.dot_general(
                chooser[...],
                outs[g].reshape(TOK, W),
                (((0,), (0,)), ((), ())),
                preferred_element_type=F32,
            )
            * weight_col
        ).reshape(NZ, 16, W)
        upd16[g] = upd16[g] + given[0]
        csend[g] = given.astype(BF16)
        for d in order:
            send(csend.at[g, d], crecv.at[g, d], zs3.at[g, d], zr3.at[g, d], zpeer(d))

    for turn in range(NG + 4):
        if turn < NG:
            add_b(turn)
        if 0 <= turn - 1 < NG:
            start_a(turn - 1)
        if 0 <= turn - 2 < NG:
            add_a(turn - 2)
        if 0 <= turn - 3 < NG:
            finish_a(turn - 3)
        if 0 <= turn - 4 < NG:
            spread(turn - 4)
    for g in range(NG):
        total = upd16[g]
        for d in reversed(order):
            arrived(crecv.at[g, d], zs3.at[g, d], zr3.at[g, d])
            total = total + crecv[g, d].astype(F32)
        for f in range(2):
            out[:, (2 * g + f) * W : (2 * g + f + 1) * W] = total[8 * f : 8 * f + 8].astype(BF16)

    for copy in sending:
        copy.wait_send()
    for d in range(1, NCTX):

        @pl.when(c + d < NCTX)
        def _():
            remote(carry.at[c], carry.at[c], carry_s.at[d], carry_r.at[d], later(d)).wait_send()
            remote(sums.at[c], sums.at[c], sum_s.at[d], sum_r.at[d], later(d)).wait_send()


def per_device(
    residual,
    mixer_input,
    mixer_gate,
    step_size,
    decay_rate,
    state_in,
    state_out,
    skip_weight,
    projection,
    norm_gain,
    routes,
    route_weight,
    up_weight,
    down_weight,
):
    vmem = pl.BlockSpec(memory_space=pltpu.VMEM)
    hbm = pl.BlockSpec(memory_space=pl.ANY)
    dma = pltpu.SemaphoreType.DMA
    scratch = [
        pltpu.VMEM((8, D), BF16),
        pltpu.VMEM((TOK, CH), BF16),
        pltpu.VMEM((TOK, CH), BF16),
        pltpu.VMEM((TOK, CH), F32),
        pltpu.VMEM((NS, CH), F32),
        pltpu.VMEM((NS, TOK), F32),
        pltpu.VMEM((NS, TOK), F32),
        pltpu.VMEM((2 * CH, D), BF16),
        pltpu.VMEM((D, 2 * FFL), BF16),
        pltpu.VMEM((2 * FFL, D), BF16),
        pltpu.VMEM((TOK, NS, CH), F32),
        pltpu.VMEM((TOK, CH), F32),
        pltpu.VMEM((TOK, CH), F32),
        pltpu.VMEM((NCTX, NS, CH), BF16),
        pltpu.VMEM((NCTX, 1, CH), F32),
        pltpu.VMEM((64, CH), BF16),
        pltpu.VMEM((64, CH), BF16),
        pltpu.VMEM((64, CH), BF16),
        pltpu.VMEM((NZ, NG, 16, W), BF16),
        pltpu.VMEM((2, 2, 16, W), BF16),
        pltpu.VMEM((2, 3, 2, 2, 16, W), BF16),
        pltpu.VMEM((NG, 16, W), F32),
        pltpu.VMEM((NG, 16, W), F32),
        pltpu.VMEM((NG, NZ, 16, W), BF16),
        pltpu.VMEM((TOK, TOK), BF16),
        pltpu.VMEM((NG, 2, 32, W), BF16),
        pltpu.VMEM((NG, 2, 32, W), BF16),
        pltpu.VMEM((4, 4, 2 * NG, 32, W), BF16),
        pltpu.VMEM((TOK, 2 * FFL), BF16),
        pltpu.VMEM((4, 4, 2 * NG, 32, W), BF16),
        pltpu.VMEM((2, 4, NG, 32, W), BF16),
        pltpu.VMEM((2, 4, 2 * NG, 32, W), BF16),
        pltpu.VMEM((2 * NG, 32, W), BF16),
        pltpu.VMEM((2, 2 * NG, 32, W), BF16),
        pltpu.VMEM((4, 2 * NG, 32, W), BF16),
        pltpu.VMEM((NG, 2, 2, 32, W), BF16),
        pltpu.VMEM((NG, NZ, 16, W), BF16),
        pltpu.VMEM((NG, NZ, 16, W), BF16),
        dma((7,)),
        dma((3,)),
        dma((3,)),
        dma((3,)),
        dma((NCTX,)),
        dma((NCTX,)),
        dma((NCTX,)),
        dma((NCTX,)),
        dma((1,)),
        dma((1,)),
        dma((NG,)),
        dma((NG,)),
        dma((NG,)),
        dma((NG,)),
        dma((2,)),
        dma((2,)),
        dma((2, 3, 2)),
        dma((2, 3, 2)),
        dma((NG, NZ)),
        dma((NG, NZ)),
        dma((NG, NZ)),
        dma((NG, NZ)),
        dma((30 * NG,)),
        dma((4, 4, 2 * NG)),
        dma((2, 4, NG)),
        dma((2, 4, NG)),
        dma((2, 4, 2 * NG)),
        dma((2, 4, 2 * NG)),
        dma((2 * NG,)),
        dma((2 * NG,)),
        dma((2, 2 * NG)),
        dma((2, 2 * NG)),
    ]
    return pl.pallas_call(
        layer_kernel,
        out_shape=jax.ShapeDtypeStruct(residual.shape, BF16),
        in_specs=[
            hbm, hbm, hbm, hbm, hbm, hbm, hbm, vmem,
            hbm, vmem, vmem, vmem, hbm, hbm,
        ],
        out_specs=vmem,
        scratch_shapes=scratch,
        compiler_params=pltpu.CompilerParams(
            collective_id=0, has_side_effects=True, vmem_limit_bytes=58 * 1024 * 1024
        ),
    )(
        residual,
        mixer_input,
        mixer_gate,
        step_size,
        decay_rate,
        state_in.T,
        state_out.T,
        skip_weight.reshape(1, CH),
        projection,
        norm_gain.reshape(1, D),
        routes.T,
        route_weight.T,
        up_weight,
        down_weight,
    )


def solution(mesh):
    in_specs = (
        P(("ctx", "exp", "half"), None),
        P("ctx", ("exp", "half")),
        P("ctx", ("exp", "half")),
        P("ctx", ("exp", "half")),
        P(None, ("exp", "half")),
        P("ctx", None),
        P("ctx", None),
        P(("exp", "half")),
        P(("exp", "half"), None),
        P(),
        P("ctx", None),
        P("ctx", None),
        P("exp", None, ("ctx", "half")),
        P("exp", ("ctx", "half"), None),
    )
    out_specs = P(("ctx", "exp", "half"), None)
    return jax.shard_map(
        per_device, mesh=mesh, in_specs=in_specs, out_specs=out_specs, check_vma=False
    )
```

```python
import jax
import jax.numpy as jnp
from jax import lax
from jax.experimental import pallas as pl
from jax.experimental.pallas import tpu as pltpu
from jax.sharding import PartitionSpec as P

F32 = jnp.float32
BF16 = jnp.bfloat16
TOK = 128
CH = 512
NS = 16
D = 4096
FFL = 384
NZ = 8
NCTX = 16
NG = 4
AHEAD = 2
W = 512
RZ = (0, 1, 2, 7, 6, 3, 4, 5)


def layer_kernel(
    residual_hbm,
    xin_hbm,
    gate_hbm,
    step_hbm,
    rate_hbm,
    sin_hbm,
    sout_hbm,
    skip,
    proj_hbm,
    gain,
    routes,
    rweight,
    up_hbm,
    down_hbm,
    out,
    residual,
    xin,
    gate,
    step,
    rate,
    sin,
    sout,
    proj,
    up,
    down,
    dec,
    drive,
    yacc,
    carry,
    sums,
    gsend,
    gmine,
    gpeer,
    psend,
    rp0,
    rp,
    own16,
    upd16,
    rows,
    chooser,
    selsend,
    selpeer,
    x,
    pre,
    hid,
    part,
    r1,
    r2,
    r4,
    qsend,
    outs,
    csend,
    crecv,
    isem,
    wsem,
    wsend,
    wrecv,
    carry_s,
    carry_r,
    sum_s,
    sum_r,
    gate_s,
    gate_r,
    sel_s,
    sel_r,
    out_s,
    out_r,
    p0_s,
    p0_r,
    p_s,
    p_r,
    zs2,
    zr2,
    zs3,
    zr3,
    ag_s,
    ag_r,
    ag_half,
    s1,
    r1s,
    s2,
    r2early,
    r2late,
    s4,
    r4s,
):
    c = lax.axis_index("ctx")
    z = lax.axis_index("exp")
    h = lax.axis_index("half")
    def remote(src, dst, ssem, rsem, to):
        return pltpu.make_async_remote_copy(
            src_ref=src,
            dst_ref=dst,
            send_sem=ssem,
            recv_sem=rsem,
            device_id=to,
            device_id_type=pl.DeviceIdType.MESH,
        )

    def send(src, dst, ssem, rsem, to):
        remote(src, dst, ssem, rsem, to).start()

    sibling = {"ctx": c, "exp": z, "half": 1 - h}

    def arrived(dst, ssem, rsem):
        remote(dst, dst, ssem, rsem, sibling).wait_recv()

    def left(src, ssem):
        remote(src, src, ssem, ssem, sibling).wait_send()

    def zpeer(d):
        return {"ctx": c, "exp": lax.rem(z + d, NZ), "half": h}

    cy, cx = lax.div(c, 4), lax.rem(c, 4)
    a = cx + h * (cy - cx)
    b = cy + h * (cx - cy)

    def ctx_at(da, db):
        return lax.rem(a + da, 4) * (1 + 3 * h) + lax.rem(b + db, 4) * (4 - 3 * h)

    def apeer(d):
        return {"ctx": ctx_at(d, 0), "exp": z, "half": h}

    def bpeer(d):
        return {"ctx": ctx_at(0, d), "exp": z, "half": h}

    inputs = [
        pltpu.make_async_copy(src, dst, isem.at[i])
        for i, (src, dst) in enumerate(
            (
                (step_hbm, step),
                (xin_hbm, xin),
                (rate_hbm, rate),
                (sin_hbm, sin),
                (sout_hbm, sout),
                (gate_hbm, gate),
                (residual_hbm, residual),
            )
        )
    ]
    local = [
        pltpu.make_async_copy(proj_hbm, proj.at[pl.ds(0, CH)], wsem.at[0]),
        pltpu.make_async_copy(up_hbm.at[0], up.at[:, pl.ds(0, FFL)], wsem.at[1]),
        pltpu.make_async_copy(down_hbm.at[0], down.at[pl.ds(0, FFL)], wsem.at[2]),
    ]
    for copy in inputs + local:
        copy.start()

    barrier = pltpu.get_barrier_semaphore()
    for d in range(1, NCTX):
        pl.semaphore_signal(
            barrier,
            inc=1,
            device_id={"ctx": lax.rem(c + d, NCTX), "exp": z, "half": h},
            device_id_type=pl.DeviceIdType.MESH,
        )
    for d in range(1, NZ):
        pl.semaphore_signal(
            barrier, inc=1, device_id=zpeer(d), device_id_type=pl.DeviceIdType.MESH
        )
    pl.semaphore_signal(
        barrier, inc=1, device_id=sibling, device_id_type=pl.DeviceIdType.MESH
    )

    for copy in inputs:
        copy.wait()
    nrate = -rate[...]
    drive[...] = step[...] * xin[...].astype(F32)
    sums[c] = jnp.sum(step[...], axis=0, keepdims=True)

    def turned(ref, base):
        return pltpu.roll(ref[...], lax.rem(TOK - base, TOK), 1)

    def first_pass(tb, state):
        base = pl.multiple_of(tb * 8, 8)
        st8 = step[pl.ds(base, 8), :]
        dr8 = drive[pl.ds(base, 8), :]
        ins = turned(sin, base)
        for i in range(8):
            decay = jnp.exp(st8[i : i + 1, :] * nrate)
            dec[base + i] = decay
            state = decay * state + dr8[i : i + 1, :] * ins[:, i : i + 1]
        return state

    zero_state = jnp.zeros((NS, CH), F32)
    carry[c] = lax.fori_loop(0, TOK // 8, first_pass, zero_state).astype(BF16)

    pl.semaphore_wait(barrier, NCTX - 1 + NZ - 1 + 1)

    def later(d):
        return {"ctx": c + d, "exp": z, "half": h}

    for d in range(1, NCTX):

        @pl.when(c + d < NCTX)
        def _():
            remote(carry.at[c], carry.at[c], carry_s.at[0], carry_r.at[0], later(d)).start()
            remote(sums.at[c], sums.at[c], sum_s.at[0], sum_r.at[0], later(d)).start()

    send(proj_hbm, proj.at[pl.ds(CH, CH)], wsend.at[0], wrecv.at[0], sibling)

    hit0 = routes[0:1, :] == z
    hit1 = routes[1:2, :] == z
    hits = jnp.where(hit0 | hit1, 1.0, 0.0).astype(F32)
    weigh = jnp.where(hit0, rweight[0:1, :], 0.0) + jnp.where(hit1, rweight[1:2, :], 0.0)
    hits = jnp.broadcast_to(hits, (TOK, TOK)).T
    weigh = jnp.broadcast_to(weigh, (TOK, TOK)).T
    major = lax.broadcasted_iota(jnp.int32, (TOK, TOK), 0)
    minor = lax.broadcasted_iota(jnp.int32, (TOK, TOK), 1)
    place = minor >> 4
    place = jnp.where(place >= 5, place - 2, jnp.where(place >= 3, 10 - place, place))
    token = 16 * ((z + place) & 7) + 8 * h + (minor & 7)
    before = jnp.sum(jnp.where(major <= token, hits, 0.0), axis=0, keepdims=True)
    same = major == token
    named = jnp.sum(jnp.where(same, hits, 0.0), axis=0, keepdims=True)
    weight_row = jnp.sum(jnp.where(same, weigh, 0.0), axis=0, keepdims=True)
    who = major >> 6
    slot = 32 * (h + who * (1 - 2 * h)) + (major & 31)
    chosen = jnp.where(
        (((major >> 5) & 1) == ((minor >> 3) & 1)) & (before == (slot + 1).astype(F32)),
        named,
        0.0,
    )
    chooser[...] = chosen.astype(BF16)
    weight_col = jnp.broadcast_to(weight_row, (TOK, TOK)).T[:, 0:1]

    for d in range(1, NCTX):

        @pl.when(c == d)
        def _():
            arrived(carry.at[pl.ds(0, d)], carry_s.at[0], carry_r.at[0])
            arrived(sums.at[pl.ds(0, d)], sum_s.at[0], sum_r.at[0])

    def enter(j, state):
        return jnp.exp(sums[j] * nrate) * state + carry[j].astype(F32)

    entering = lax.fori_loop(0, c, enter, zero_state)

    def second_pass(tb, state):
        base = pl.multiple_of(tb * 8, 8)
        dr8 = drive[pl.ds(base, 8), :]
        ins = turned(sin, base)
        outw = turned(sout, base)
        for i in range(8):
            state = dec[base + i] * state + dr8[i : i + 1, :] * ins[:, i : i + 1]
            yacc[pl.ds(base + i, 1), :] = jnp.sum(
                state * outw[:, i : i + 1], axis=0, keepdims=True
            )
        return state

    lax.fori_loop(0, TOK // 8, second_pass, entering)

    gates = gate[...].astype(F32)
    yacc[...] = (yacc[...] + skip[...] * xin[...].astype(F32)) * (
        gates / (1.0 + jnp.exp(-gates))
    )

    def eights(whose):
        return jnp.concatenate(
            [
                yacc[pl.ds(pl.multiple_of(16 * lax.rem(z + d, NZ) + 8 * whose, 8), 8), :]
                for d in range(NZ)
            ],
            axis=0,
        ).astype(BF16)

    gsend[...] = eights(1 - h)
    send(gsend, gpeer, gate_s.at[0], gate_r.at[0], sibling)
    send(up_hbm.at[0], up.at[:, pl.ds(FFL, FFL)], wsend.at[1], wrecv.at[1], sibling)
    send(down_hbm.at[0], down.at[pl.ds(FFL, FFL)], wsend.at[2], wrecv.at[2], sibling)
    gmine[...] = eights(h)

    local[0].wait()
    arrived(proj.at[pl.ds(CH, CH)], wsend.at[0], wrecv.at[0])
    arrived(gpeer, gate_s.at[0], gate_r.at[0])

    def project(g, _):
        def block(f):
            cols = pl.ds(pl.multiple_of((2 * g + f) * W, W), W)
            return (
                jnp.dot(gmine[...], proj[0:CH, cols], preferred_element_type=F32)
                + jnp.dot(gpeer[...], proj[CH : 2 * CH, cols], preferred_element_type=F32)
            ).reshape(NZ, 8, W)

        both = jnp.concatenate([block(0), block(1)], axis=1)
        own16[g] = both[0]
        psend[:, g] = both.astype(BF16)
        return 0

    lax.fori_loop(0, NG, project, 0)

    def ring(way, pos, half, slot):
        send(
            psend.at[pos, pl.ds(2 * half, 2)],
            rp.at[way, slot, half],
            p_s.at[0],
            p_r.at[way, slot, half],
            zpeer(1) if way == 0 else zpeer(NZ - 1),
        )

    def add_in(pos, half, got):
        mine = psend[pos, 2 * half : 2 * half + 2].astype(F32)
        psend[pos, 2 * half : 2 * half + 2] = (mine + got.astype(F32)).astype(BF16)

    for way in range(2):
        send(
            psend.at[4, pl.ds(2 * way, 2)],
            rp0.at[way],
            p0_s.at[0],
            p0_r.at[way],
            zpeer(1) if way == 0 else zpeer(NZ - 1),
        )
    for way in range(2):
        ring(way, 3 if way == 0 else 5, 1 - way, 0)
    for way in range(2):
        arrived(rp0.at[way], p0_s.at[0], p0_r.at[way])
        pos = 3 if way == 0 else 5
        add_in(pos, way, rp0[way])
        ring(way, pos, way, 0)
    for slot in range(2):
        for turn in range(2):
            for way in range(2):
                half = 1 - way if turn == 0 else way
                arrived(rp.at[way, slot, half], p_s.at[0], p_r.at[way, slot, half])
                pos = 2 - slot if way == 0 else 6 + slot
                add_in(pos, half, rp[way, slot, half])
                ring(way, pos, half, slot + 1)
    squares = jnp.zeros((16, 1), F32)
    for half in range(2):
        for way in range(2):
            arrived(rp.at[way, 2, half], p_s.at[0], p_r.at[way, 2, half])
    for g in range(NG):
        res = residual[:, 2 * W * g : 2 * W * (g + 1)].astype(F32)
        total = own16[g] + jnp.concatenate([res[:, :W], res[:, W:]], axis=0)
        for way in range(2):
            total = total + rp[way, 2, g // 2, g % 2].astype(F32)
        upd16[g] = total
        squares = squares + jnp.sum(total * total, axis=1, keepdims=True)

    scale = lax.rsqrt((squares[0:8] + squares[8:16]) * (1.0 / D) + 1e-05)
    scale = jnp.concatenate([scale, scale], axis=0)
    far_first = (6, 5, 7, 4, 2, 3, 1)

    def send_rows(g):
        for i in far_first:
            near = 0 if RZ.index(NZ - RZ[i]) < 5 else 1
            send(
                rows.at[0, g],
                rows.at[RZ.index(NZ - RZ[i]), g],
                zs2.at[0],
                zr2.at[g, near],
                zpeer(RZ[i]),
            )

    for g in range(NG):
        gains = jnp.concatenate(
            [
                jnp.broadcast_to(gain[:, (2 * g + f) * W : (2 * g + f + 1) * W], (8, W))
                for f in range(2)
            ],
            axis=0,
        )
        rows[0, g] = (upd16[g] * scale * gains).astype(BF16)
        if g < AHEAD:
            send_rows(g)

    def select(g):
        arrived(rows.at[pl.ds(1, 4), g], zs2.at[0], zr2.at[g, 0])
        if g + AHEAD < NG:
            send_rows(g + AHEAD)
        arrived(rows.at[pl.ds(5, 3), g], zs2.at[0], zr2.at[g, 1])
        picked = jnp.dot(
            chooser[...], rows[:, g].reshape(TOK, W), preferred_element_type=F32
        )
        selsend[g] = picked[64:128].astype(BF16).reshape(2, 32, W)
        send(selsend.at[g], selpeer.at[g], sel_s.at[0], sel_r.at[g], sibling)
        arrived(selpeer.at[g], sel_s.at[0], sel_r.at[g])
        x[0, 2 * g : 2 * g + 2] = (
            picked[0:64].reshape(2, 32, W) + selpeer[g].astype(F32)
        ).astype(BF16)

    def pair(g):
        return pl.ds(2 * g, 2)

    def ready(rb, ra, g):
        return ag_r.at[(8 if rb == 3 else 4 * rb) + ra, g]

    def gather(ra, g, to, lb, la):
        send(x.at[ra, pair(g)], x.at[4 * lb + la, pair(g)], ag_s.at[0], ready(lb, la, g), to)

    def have(rb, ra, g):
        arrived(x.at[4 * rb + ra, pair(g)], ag_s.at[0], ready(rb, ra, g))

    def along_b(ra, g):
        gather(ra, g, bpeer(1), 3, ra)
        gather(ra, g, bpeer(3), 1, ra)

    def begin(g):
        for d in (2, 1, 3):
            gather(0, g, apeer(d), 0, 4 - d)
        along_b(0, g)

    def neighbours(g):
        for ra in (3, 1, 2):
            have(0, ra, g)
            along_b(ra, g)

    def pass_on(g):
        for ra in (0, 3, 1, 2):
            for side in range(2):
                rb, e = 3 - 2 * side, 2 * g + side
                have(rb, ra, g)
                send(
                    x.at[4 * rb + ra, e],
                    x.at[8 + ra, e],
                    ag_s.at[0],
                    ag_half.at[ra, e],
                    bpeer(1 + 2 * side),
                )

    def widen(rb, g):
        wide = jnp.concatenate(
            [x[4 * rb : 4 * rb + 4, e].reshape(TOK, W) for e in (2 * g, 2 * g + 1)], axis=1
        )
        got = jnp.dot(wide, up[2 * g * W : 2 * (g + 1) * W, :], preferred_element_type=F32)
        if g == 0:
            pre[rb] = got
        elif g < NG - 1:
            pre[rb] = pre[rb] + got
        else:
            got = pre[rb] + got
            hid[...] = (got / (1.0 + jnp.exp(-got))).astype(BF16)

    for turn in range(NG):
        select(turn)
        begin(turn)
        if turn == 0:
            local[1].wait()
            local[2].wait()
            arrived(up.at[:, pl.ds(FFL, FFL)], wsend.at[1], wrecv.at[1])
            arrived(down.at[pl.ds(FFL, FFL)], wsend.at[2], wrecv.at[2])
        if turn >= 1:
            neighbours(turn - 1)
            widen(0, turn - 1)
        if turn >= 2:
            pass_on(turn - 2)
            widen(1, turn - 2)
            widen(3, turn - 2)
    neighbours(NG - 1)
    pass_on(NG - 2)

    def narrow(rb, g):
        for e in (2 * g, 2 * g + 1):
            part[rb, :, e] = (
                jnp.dot(hid[...], down[:, e * W : (e + 1) * W], preferred_element_type=F32)
                .astype(BF16)
                .reshape(4, 32, W)
            )

    turns = (2, 1, 3, 0)
    widen(0, NG - 1)
    for g in range(NG):
        narrow(0, g)
    widen(1, NG - 2)
    widen(3, NG - 2)
    pass_on(NG - 1)
    for side in range(2):
        widen(1 + 2 * side, NG - 1)
        for g in range(NG):
            e = 2 * g + 1 - side
            narrow(1 + 2 * side, g)
            send(
                part.at[1 + 2 * side, pl.ds(0, 4), e],
                r2.at[side, pl.ds(0, 4), e],
                s2.at[0],
                r2early.at[side, g],
                bpeer(1 + 2 * side),
            )
    for g in range(NG):
        for ra in range(4):
            for e in (2 * g, 2 * g + 1):
                arrived(x.at[8 + ra, e], ag_s.at[0], ag_half.at[ra, e])
        widen(2, g)
    for g in range(NG):
        narrow(2, g)
        for side in range(2):
            send(
                part.at[2, pl.ds(0, 4), 2 * g + side],
                r1.at[side, pl.ds(0, 4), g],
                s1.at[0],
                r1s.at[side, g],
                bpeer(1 + 2 * side),
            )

    def add_b(g):
        for side in range(2):
            arrived(r1.at[side, pl.ds(0, 4), g], s1.at[0], r1s.at[side, g])
        for ra in turns:
            for side in range(2):
                e = 2 * g + side
                part[1 + 2 * side, ra, e] = (
                    part[1 + 2 * side, ra, e].astype(F32) + r1[side, ra, g].astype(F32)
                ).astype(BF16)
                send(
                    part.at[1 + 2 * side, ra, e],
                    r2.at[side, ra, e],
                    s2.at[0],
                    r2late.at[side, ra, g],
                    bpeer(1 + 2 * side),
                )

    def summed_b(ra, g):
        total = part[0, ra, 2 * g : 2 * g + 2].astype(F32)
        for side in range(2):
            arrived(r2.at[side, ra, 2 * g + side], s2.at[0], r2late.at[side, ra, g])
            total = total + r2[side, ra, 2 * g : 2 * g + 2].astype(F32)
        return total

    def start_a(g):
        for side in range(2):
            e = 2 * g + 1 - side
            arrived(r2.at[side, pl.ds(0, 4), e], s2.at[0], r2early.at[side, g])
        for ra in (2, 1, 3):
            qsend[ra - 1, 2 * g : 2 * g + 2] = summed_b(ra, g).astype(BF16)
            send(
                qsend.at[ra - 1, pair(g)],
                r4.at[ra - 1, pair(g)],
                s4.at[0],
                r4s.at[ra - 1, g],
                apeer(ra),
            )

    def finish_a(g):
        total = summed_b(0, g)
        for i in range(3):
            arrived(r4.at[i, pair(g)], s4.at[0], r4s.at[i, g])
            total = total + r4[i, 2 * g : 2 * g + 2].astype(F32)
        outs[g, 0] = total.astype(BF16)
        send(outs.at[g, 0], outs.at[g, 1], out_s.at[0], out_r.at[g], sibling)

    def spread(g):
        arrived(outs.at[g, 1], out_s.at[0], out_r.at[g])
        given = (
            lax.dot_general(
                chooser[...],
                outs[g].reshape(TOK, W),
                (((0,), (0,)), ((), ())),
                preferred_element_type=F32,
            )
            * weight_col
        ).reshape(NZ, 16, W)
        upd16[g] = upd16[g] + given[0]
        csend[:, g] = given.astype(BF16)
        for i in far_first:
            send(csend.at[i, g], crecv.at[i, g], zs3.at[0], zr3.at[g], zpeer(RZ[i]))

    for g in range(NG):
        add_b(g)
    for turn in range(NG + 3):
        if turn < NG:
            start_a(turn)
        if 0 <= turn - 2 < NG:
            finish_a(turn - 2)
        if 0 <= turn - 3 < NG:
            spread(turn - 3)
    for g in range(NG):
        arrived(crecv.at[pl.ds(1, NZ - 1), g], zs3.at[0], zr3.at[g])
        total = upd16[g]
        for i in range(1, NZ):
            total = total + crecv[i, g].astype(F32)
        for f in range(2):
            out[:, (2 * g + f) * W : (2 * g + f + 1) * W] = total[8 * f : 8 * f + 8].astype(BF16)

    left(proj.at[pl.ds(0, CH)], wsend.at[0])
    left(up.at[:, pl.ds(0, FFL)], wsend.at[1])
    left(down.at[pl.ds(0, FFL)], wsend.at[2])
    for d in range(1, NCTX):

        @pl.when(c + d == NCTX - 1)
        def _():
            left(carry.at[pl.ds(0, d)], carry_s.at[0])
            left(sums.at[pl.ds(0, d)], sum_s.at[0])

    left(gsend, gate_s.at[0])
    left(rp0, p0_s.at[0])
    left(rp, p_s.at[0])
    left(rows.at[pl.ds(1, NZ - 1)], zs2.at[0])
    left(selsend, sel_s.at[0])
    left(x.at[pl.ds(0, 15)], ag_s.at[0])
    left(r1, s1.at[0])
    left(r2, s2.at[0])
    left(r4, s4.at[0])
    left(selsend, out_s.at[0])
    left(crecv.at[pl.ds(1, NZ - 1)], zs3.at[0])


def per_device(
    residual,
    mixer_input,
    mixer_gate,
    step_size,
    decay_rate,
    state_in,
    state_out,
    skip_weight,
    projection,
    norm_gain,
    routes,
    route_weight,
    up_weight,
    down_weight,
):
    vmem = pl.BlockSpec(memory_space=pltpu.VMEM)
    hbm = pl.BlockSpec(memory_space=pl.ANY)
    dma = pltpu.SemaphoreType.DMA
    scratch = [
        pltpu.VMEM((8, D), BF16),
        pltpu.VMEM((TOK, CH), BF16),
        pltpu.VMEM((TOK, CH), BF16),
        pltpu.VMEM((TOK, CH), F32),
        pltpu.VMEM((NS, CH), F32),
        pltpu.VMEM((NS, TOK), F32),
        pltpu.VMEM((NS, TOK), F32),
        pltpu.VMEM((2 * CH, D), BF16),
        pltpu.VMEM((D, 2 * FFL), BF16),
        pltpu.VMEM((2 * FFL, D), BF16),
        pltpu.VMEM((TOK, NS, CH), F32),
        pltpu.VMEM((TOK, CH), F32),
        pltpu.VMEM((TOK, CH), F32),
        pltpu.VMEM((NCTX, NS, CH), BF16),
        pltpu.VMEM((NCTX, 1, CH), F32),
        pltpu.VMEM((64, CH), BF16),
        pltpu.VMEM((64, CH), BF16),
        pltpu.VMEM((64, CH), BF16),
        pltpu.VMEM((NZ, NG, 16, W), BF16),
        pltpu.VMEM((2, 2, 16, W), BF16),
        pltpu.VMEM((2, 3, 2, 2, 16, W), BF16),
        pltpu.VMEM((NG, 16, W), F32),
        pltpu.VMEM((NG, 16, W), F32),
        pltpu.VMEM((NZ, NG, 16, W), BF16),
        pltpu.VMEM((TOK, TOK), BF16),
        pltpu.VMEM((NG, 2, 32, W), BF16),
        pltpu.VMEM((NG, 2, 32, W), BF16),
        pltpu.VMEM((16, 2 * NG, 32, W), BF16),
        pltpu.VMEM((4, TOK, 2 * FFL), F32),
        pltpu.VMEM((TOK, 2 * FFL), BF16),
        pltpu.VMEM((4, 4, 2 * NG, 32, W), BF16),
        pltpu.VMEM((2, 4, NG, 32, W), BF16),
        pltpu.VMEM((2, 4, 2 * NG, 32, W), BF16),
        pltpu.VMEM((3, 2 * NG, 32, W), BF16),
        pltpu.VMEM((3, 2 * NG, 32, W), BF16),
        pltpu.VMEM((NG, 2, 2, 32, W), BF16),
        pltpu.VMEM((NZ, NG, 16, W), BF16),
        pltpu.VMEM((NZ, NG, 16, W), BF16),
        dma((7,)),
        dma((3,)),
        dma((3,)),
        dma((3,)),
        dma((1,)),
        dma((1,)),
        dma((1,)),
        dma((1,)),
        dma((1,)),
        dma((1,)),
        dma((1,)),
        dma((NG,)),
        dma((1,)),
        dma((NG,)),
        dma((1,)),
        dma((2,)),
        dma((1,)),
        dma((2, 3, 2)),
        dma((1,)),
        dma((NG, 2)),
        dma((1,)),
        dma((NG,)),
        dma((1,)),
        dma((12, NG)),
        dma((4, 2 * NG)),
        dma((1,)),
        dma((2, NG)),
        dma((1,)),
        dma((2, NG)),
        dma((2, 4, NG)),
        dma((1,)),
        dma((3, NG)),
    ]
    return pl.pallas_call(
        layer_kernel,
        out_shape=jax.ShapeDtypeStruct(residual.shape, BF16),
        in_specs=[
            hbm, hbm, hbm, hbm, hbm, hbm, hbm, vmem,
            hbm, vmem, vmem, vmem, hbm, hbm,
        ],
        out_specs=vmem,
        scratch_shapes=scratch,
        compiler_params=pltpu.CompilerParams(
            collective_id=0, has_side_effects=True, vmem_limit_bytes=58 * 1024 * 1024
        ),
    )(
        residual,
        mixer_input,
        mixer_gate,
        step_size,
        decay_rate,
        state_in.T,
        state_out.T,
        skip_weight.reshape(1, CH),
        projection,
        norm_gain.reshape(1, D),
        routes.T,
        route_weight.T,
        up_weight,
        down_weight,
    )


def solution(mesh):
    in_specs = (
        P(("ctx", "exp", "half"), None),
        P("ctx", ("exp", "half")),
        P("ctx", ("exp", "half")),
        P("ctx", ("exp", "half")),
        P(None, ("exp", "half")),
        P("ctx", None),
        P("ctx", None),
        P(("exp", "half")),
        P(("exp", "half"), None),
        P(),
        P("ctx", None),
        P("ctx", None),
        P("exp", None, ("ctx", "half")),
        P("exp", ("ctx", "half"), None),
    )
    out_specs = P(("ctx", "exp", "half"), None)
    return jax.shard_map(
        per_device, mesh=mesh, in_specs=in_specs, out_specs=out_specs, check_vma=False
    )
```

```python
import jax
import jax.numpy as jnp
from jax import lax
from jax.experimental import pallas as pl
from jax.experimental.pallas import tpu as pltpu
from jax.sharding import PartitionSpec as P

F32 = jnp.float32
BF16 = jnp.bfloat16
TOK = 128
CH = 512
NS = 16
D = 4096
FFL = 384
NZ = 8
NCTX = 16
NG = 4
AHEAD = 2
W = 512
RZ = (0, 1, 2, 7, 6, 3, 4, 5)


def layer_kernel(
    residual_hbm,
    xin_hbm,
    gate_hbm,
    step_hbm,
    rate_hbm,
    sin_hbm,
    sout_hbm,
    skip,
    proj_hbm,
    gain,
    routes,
    rweight,
    up_hbm,
    down_hbm,
    out,
    residual,
    xin,
    gate,
    step,
    rate,
    sin,
    sout,
    proj,
    up,
    down,
    dec,
    drive,
    yacc,
    carry,
    sums,
    gsend,
    gmine,
    gpeer,
    psend,
    rp0,
    rp,
    own16,
    upd16,
    rows,
    chooser,
    selsend,
    selpeer,
    x,
    pre,
    hid,
    part,
    r1,
    r2,
    r4,
    qsend,
    outs,
    csend,
    crecv,
    isem,
    wsem,
    wsend,
    wrecv,
    carry_s,
    carry_r,
    sum_s,
    sum_r,
    gate_s,
    gate_r,
    sel_s,
    sel_r,
    out_s,
    out_r,
    p0_s,
    p0_r,
    p_s,
    p_r,
    zs2,
    zr2,
    zs3,
    zr3,
    ag_s,
    ag_r,
    ag_half,
    s1,
    r1s,
    s2,
    r2early,
    r2late,
    s4,
    r4s,
):
    c = lax.axis_index("ctx")
    z = lax.axis_index("exp")
    h = lax.axis_index("half")
    def remote(src, dst, ssem, rsem, to):
        return pltpu.make_async_remote_copy(
            src_ref=src,
            dst_ref=dst,
            send_sem=ssem,
            recv_sem=rsem,
            device_id=to,
            device_id_type=pl.DeviceIdType.MESH,
        )

    def send(src, dst, ssem, rsem, to):
        remote(src, dst, ssem, rsem, to).start()

    sibling = {"ctx": c, "exp": z, "half": 1 - h}

    def arrived(dst, ssem, rsem):
        remote(dst, dst, ssem, rsem, sibling).wait_recv()

    def left(src, ssem):
        remote(src, src, ssem, ssem, sibling).wait_send()

    def zpeer(d):
        return {"ctx": c, "exp": lax.rem(z + d, NZ), "half": h}

    cy, cx = lax.div(c, 4), lax.rem(c, 4)
    a = cx + h * (cy - cx)
    b = cy + h * (cx - cy)

    def ctx_at(da, db):
        return lax.rem(a + da, 4) * (1 + 3 * h) + lax.rem(b + db, 4) * (4 - 3 * h)

    def apeer(d):
        return {"ctx": ctx_at(d, 0), "exp": z, "half": h}

    def bpeer(d):
        return {"ctx": ctx_at(0, d), "exp": z, "half": h}

    inputs = [
        pltpu.make_async_copy(src, dst, isem.at[i])
        for i, (src, dst) in enumerate(
            (
                (step_hbm, step),
                (xin_hbm, xin),
                (rate_hbm, rate),
                (sin_hbm, sin),
                (sout_hbm, sout),
                (gate_hbm, gate),
                (residual_hbm, residual),
            )
        )
    ]
    local = [
        pltpu.make_async_copy(proj_hbm, proj.at[pl.ds(0, CH)], wsem.at[0]),
        pltpu.make_async_copy(up_hbm.at[0], up.at[:, pl.ds(0, FFL)], wsem.at[1]),
        pltpu.make_async_copy(down_hbm.at[0], down.at[pl.ds(0, FFL)], wsem.at[2]),
    ]
    for copy in inputs + local:
        copy.start()

    barrier = pltpu.get_barrier_semaphore()
    for d in range(1, NCTX):
        pl.semaphore_signal(
            barrier,
            inc=1,
            device_id={"ctx": lax.rem(c + d, NCTX), "exp": z, "half": h},
            device_id_type=pl.DeviceIdType.MESH,
        )
    for d in range(1, NZ):
        pl.semaphore_signal(
            barrier, inc=1, device_id=zpeer(d), device_id_type=pl.DeviceIdType.MESH
        )
    pl.semaphore_signal(
        barrier, inc=1, device_id=sibling, device_id_type=pl.DeviceIdType.MESH
    )

    for copy in inputs:
        copy.wait()
    nrate = -rate[...]
    drive[...] = step[...] * xin[...].astype(F32)
    sums[c] = jnp.sum(step[...], axis=0, keepdims=True)

    def turned(ref, base):
        return pltpu.roll(ref[...], lax.rem(TOK - base, TOK), 1)

    def first_pass(tb, state):
        base = pl.multiple_of(tb * 8, 8)
        st8 = step[pl.ds(base, 8), :]
        dr8 = drive[pl.ds(base, 8), :]
        ins = turned(sin, base)
        for i in range(8):
            decay = jnp.exp(st8[i : i + 1, :] * nrate)
            dec[base + i] = decay
            state = decay * state + dr8[i : i + 1, :] * ins[:, i : i + 1]
        return state

    zero_state = jnp.zeros((NS, CH), F32)
    carry[c] = lax.fori_loop(0, TOK // 8, first_pass, zero_state).astype(BF16)

    pl.semaphore_wait(barrier, NCTX - 1 + NZ - 1 + 1)

    def later(d):
        return {"ctx": c + d, "exp": z, "half": h}

    for d in range(1, NCTX):

        @pl.when(c + d < NCTX)
        def _():
            remote(carry.at[c], carry.at[c], carry_s.at[0], carry_r.at[0], later(d)).start()
            remote(sums.at[c], sums.at[c], sum_s.at[0], sum_r.at[0], later(d)).start()

    send(proj_hbm, proj.at[pl.ds(CH, CH)], wsend.at[0], wrecv.at[0], sibling)

    hit0 = routes[0:1, :] == z
    hit1 = routes[1:2, :] == z
    hits = jnp.where(hit0 | hit1, 1.0, 0.0).astype(F32)
    weigh = jnp.where(hit0, rweight[0:1, :], 0.0) + jnp.where(hit1, rweight[1:2, :], 0.0)
    hits = jnp.broadcast_to(hits, (TOK, TOK)).T
    weigh = jnp.broadcast_to(weigh, (TOK, TOK)).T
    major = lax.broadcasted_iota(jnp.int32, (TOK, TOK), 0)
    minor = lax.broadcasted_iota(jnp.int32, (TOK, TOK), 1)
    place = minor >> 4
    place = jnp.where(place >= 5, place - 2, jnp.where(place >= 3, 10 - place, place))
    token = 16 * ((z + place) & 7) + 8 * h + (minor & 7)
    before = jnp.sum(jnp.where(major <= token, hits, 0.0), axis=0, keepdims=True)
    same = major == token
    named = jnp.sum(jnp.where(same, hits, 0.0), axis=0, keepdims=True)
    weight_row = jnp.sum(jnp.where(same, weigh, 0.0), axis=0, keepdims=True)
    who = major >> 6
    slot = 32 * (h + who * (1 - 2 * h)) + (major & 31)
    chosen = jnp.where(
        (((major >> 5) & 1) == ((minor >> 3) & 1)) & (before == (slot + 1).astype(F32)),
        named,
        0.0,
    )
    chooser[...] = chosen.astype(BF16)
    weight_col = jnp.broadcast_to(weight_row, (TOK, TOK)).T[:, 0:1]

    for d in range(1, NCTX):

        @pl.when(c == d)
        def _():
            arrived(carry.at[pl.ds(0, d)], carry_s.at[0], carry_r.at[0])
            arrived(sums.at[pl.ds(0, d)], sum_s.at[0], sum_r.at[0])

    def enter(j, state):
        return jnp.exp(sums[j] * nrate) * state + carry[j].astype(F32)

    entering = lax.fori_loop(0, c, enter, zero_state)

    def second_pass(tb, state):
        base = pl.multiple_of(tb * 8, 8)
        dr8 = drive[pl.ds(base, 8), :]
        ins = turned(sin, base)
        outw = turned(sout, base)
        for i in range(8):
            state = dec[base + i] * state + dr8[i : i + 1, :] * ins[:, i : i + 1]
            yacc[pl.ds(base + i, 1), :] = jnp.sum(
                state * outw[:, i : i + 1], axis=0, keepdims=True
            )
        return state

    lax.fori_loop(0, TOK // 8, second_pass, entering)

    gates = gate[...].astype(F32)
    yacc[...] = (yacc[...] + skip[...] * xin[...].astype(F32)) * (
        gates / (1.0 + jnp.exp(-gates))
    )

    def eights(whose):
        return jnp.concatenate(
            [
                yacc[pl.ds(pl.multiple_of(16 * lax.rem(z + d, NZ) + 8 * whose, 8), 8), :]
                for d in range(NZ)
            ],
            axis=0,
        ).astype(BF16)

    gsend[...] = eights(1 - h)
    send(gsend, gpeer, gate_s.at[0], gate_r.at[0], sibling)
    send(up_hbm.at[0], up.at[:, pl.ds(FFL, FFL)], wsend.at[1], wrecv.at[1], sibling)
    send(down_hbm.at[0], down.at[pl.ds(FFL, FFL)], wsend.at[2], wrecv.at[2], sibling)
    gmine[...] = eights(h)

    local[0].wait()
    arrived(proj.at[pl.ds(CH, CH)], wsend.at[0], wrecv.at[0])
    arrived(gpeer, gate_s.at[0], gate_r.at[0])

    def project(g, _):
        def block(f):
            cols = pl.ds(pl.multiple_of((2 * g + f) * W, W), W)
            return (
                jnp.dot(gmine[...], proj[0:CH, cols], preferred_element_type=F32)
                + jnp.dot(gpeer[...], proj[CH : 2 * CH, cols], preferred_element_type=F32)
            ).reshape(NZ, 8, W)

        both = jnp.concatenate([block(0), block(1)], axis=1)
        own16[g] = both[0]
        psend[:, g] = both.astype(BF16)
        return 0

    lax.fori_loop(0, NG, project, 0)

    for way in range(2):
        send(
            psend.at[4, pl.ds(2 * way, 2)],
            rp0.at[way],
            p0_s.at[0],
            p0_r.at[way],
            zpeer((2, 6)[way]),
        )
        send(psend.at[(3, 5)[way]], rp.at[way, 0], p_s.at[0], p_r.at[way, 0], zpeer((1, 7)[way]))
    for way in range(2):
        send(psend.at[(1, 7)[way]], rp.at[way, 1], p_s.at[0], p_r.at[way, 1], zpeer((1, 7)[way]))
    for way in range(2):
        pos = (2, 6)[way]
        arrived(rp.at[way, 0], p_s.at[0], p_r.at[way, 0])
        arrived(rp0.at[way], p0_s.at[0], p0_r.at[way])
        for g in range(NG):
            total = psend[pos, g].astype(F32) + rp[way, 0, g].astype(F32)
            if g // 2 == way:
                total = total + rp0[way, g % 2].astype(F32)
            psend[pos, g] = total.astype(BF16)
        send(psend.at[pos], rp.at[way, 2], p_s.at[0], p_r.at[way, 2], zpeer(pos))
    for way in range(2):
        for slot in (1, 2):
            arrived(rp.at[way, slot], p_s.at[0], p_r.at[way, slot])
    squares = jnp.zeros((16, 1), F32)
    for g in range(NG):
        res = residual[:, 2 * W * g : 2 * W * (g + 1)].astype(F32)
        total = own16[g] + jnp.concatenate([res[:, :W], res[:, W:]], axis=0)
        for way in range(2):
            total = total + rp[way, 1, g].astype(F32) + rp[way, 2, g].astype(F32)
        upd16[g] = total
        squares = squares + jnp.sum(total * total, axis=1, keepdims=True)

    scale = lax.rsqrt((squares[0:8] + squares[8:16]) * (1.0 / D) + 1e-05)
    scale = jnp.concatenate([scale, scale], axis=0)
    far_first = (6, 5, 7, 4, 2, 3, 1)

    def send_rows(g):
        for i in far_first:
            near = 0 if RZ.index(NZ - RZ[i]) < 5 else 1
            send(
                rows.at[0, g],
                rows.at[RZ.index(NZ - RZ[i]), g],
                zs2.at[0],
                zr2.at[g, near],
                zpeer(RZ[i]),
            )

    for g in range(NG):
        gains = jnp.concatenate(
            [
                jnp.broadcast_to(gain[:, (2 * g + f) * W : (2 * g + f + 1) * W], (8, W))
                for f in range(2)
            ],
            axis=0,
        )
        rows[0, g] = (upd16[g] * scale * gains).astype(BF16)
        if g < AHEAD:
            send_rows(g)

    def select(g):
        arrived(rows.at[pl.ds(1, 4), g], zs2.at[0], zr2.at[g, 0])
        if g + AHEAD < NG:
            send_rows(g + AHEAD)
        arrived(rows.at[pl.ds(5, 3), g], zs2.at[0], zr2.at[g, 1])
        picked = jnp.dot(
            chooser[...], rows[:, g].reshape(TOK, W), preferred_element_type=F32
        )
        selsend[g] = picked[64:128].astype(BF16).reshape(2, 32, W)
        send(selsend.at[g], selpeer.at[g], sel_s.at[0], sel_r.at[g], sibling)
        arrived(selpeer.at[g], sel_s.at[0], sel_r.at[g])
        x[0, 2 * g : 2 * g + 2] = (
            picked[0:64].reshape(2, 32, W) + selpeer[g].astype(F32)
        ).astype(BF16)

    def pair(g):
        return pl.ds(2 * g, 2)

    def ready(rb, ra, g):
        return ag_r.at[(8 if rb == 3 else 4 * rb) + ra, g]

    def gather(ra, g, to, lb, la):
        send(x.at[ra, pair(g)], x.at[4 * lb + la, pair(g)], ag_s.at[0], ready(lb, la, g), to)

    def have(rb, ra, g):
        arrived(x.at[4 * rb + ra, pair(g)], ag_s.at[0], ready(rb, ra, g))

    def along_b(ra, g):
        gather(ra, g, bpeer(1), 3, ra)
        gather(ra, g, bpeer(3), 1, ra)

    def begin(g):
        for d in (2, 1, 3):
            gather(0, g, apeer(d), 0, 4 - d)
        along_b(0, g)

    def neighbours(g):
        for ra in (3, 1, 2):
            have(0, ra, g)
            along_b(ra, g)

    def pass_on(g):
        for ra in (0, 3, 1, 2):
            for side in range(2):
                rb, e = 3 - 2 * side, 2 * g + side
                have(rb, ra, g)
                send(
                    x.at[4 * rb + ra, e],
                    x.at[8 + ra, e],
                    ag_s.at[0],
                    ag_half.at[ra, e],
                    bpeer(1 + 2 * side),
                )

    def widen(rb, g):
        wide = jnp.concatenate(
            [x[4 * rb : 4 * rb + 4, e].reshape(TOK, W) for e in (2 * g, 2 * g + 1)], axis=1
        )
        got = jnp.dot(wide, up[2 * g * W : 2 * (g + 1) * W, :], preferred_element_type=F32)
        if g == 0:
            pre[rb] = got
        elif g < NG - 1:
            pre[rb] = pre[rb] + got
        else:
            got = pre[rb] + got
            hid[...] = (got / (1.0 + jnp.exp(-got))).astype(BF16)

    for turn in range(NG):
        select(turn)
        begin(turn)
        if turn == 0:
            local[1].wait()
            local[2].wait()
            arrived(up.at[:, pl.ds(FFL, FFL)], wsend.at[1], wrecv.at[1])
            arrived(down.at[pl.ds(FFL, FFL)], wsend.at[2], wrecv.at[2])
        if turn >= 1:
            neighbours(turn - 1)
            widen(0, turn - 1)
        if turn >= 2:
            pass_on(turn - 2)
            widen(1, turn - 2)
            widen(3, turn - 2)
    neighbours(NG - 1)
    pass_on(NG - 2)

    def narrow(rb, g):
        for e in (2 * g, 2 * g + 1):
            part[rb, :, e] = (
                jnp.dot(hid[...], down[:, e * W : (e + 1) * W], preferred_element_type=F32)
                .astype(BF16)
                .reshape(4, 32, W)
            )

    widen(0, NG - 1)
    for g in range(NG):
        narrow(0, g)
    widen(1, NG - 2)
    widen(3, NG - 2)
    pass_on(NG - 1)
    for side in range(2):
        widen(1 + 2 * side, NG - 1)
        for g in range(NG):
            e = 2 * g + 1 - side
            narrow(1 + 2 * side, g)
            send(
                part.at[1 + 2 * side, pl.ds(0, 4), e],
                r2.at[side, pl.ds(0, 4), e],
                s2.at[0],
                r2early.at[side, g],
                bpeer(1 + 2 * side),
            )
    for g in range(NG):
        for ra in range(4):
            for e in (2 * g, 2 * g + 1):
                arrived(x.at[8 + ra, e], ag_s.at[0], ag_half.at[ra, e])
        widen(2, g)
    for g in range(NG):
        narrow(2, g)
        for side in range(2):
            send(
                part.at[2, pl.ds(0, 4), 2 * g + side],
                r1.at[side, pl.ds(0, 4), g],
                s1.at[0],
                r1s.at[side, g],
                bpeer(1 + 2 * side),
            )

    def add_b(g):
        for side in range(2):
            arrived(r1.at[side, pl.ds(0, 4), g], s1.at[0], r1s.at[side, g])
        for side in range(2):
            e = 2 * g + side
            part[1 + 2 * side, :, e] = (
                part[1 + 2 * side, :, e].astype(F32) + r1[side, :, g].astype(F32)
            ).astype(BF16)
            send(
                part.at[1 + 2 * side, pl.ds(0, 4), e],
                r2.at[side, pl.ds(0, 4), e],
                s2.at[0],
                r2late.at[side, g],
                bpeer(1 + 2 * side),
            )

    def summed_b(ra, g):
        total = part[0, ra, 2 * g : 2 * g + 2].astype(F32)
        for side in range(2):
            total = total + r2[side, ra, 2 * g : 2 * g + 2].astype(F32)
        return total

    def start_a(g):
        for side in range(2):
            e = 2 * g + 1 - side
            arrived(r2.at[side, pl.ds(0, 4), e], s2.at[0], r2early.at[side, g])
            e = 2 * g + side
            arrived(r2.at[side, pl.ds(0, 4), e], s2.at[0], r2late.at[side, g])
        for ra in (2, 1, 3):
            qsend[ra - 1, 2 * g : 2 * g + 2] = summed_b(ra, g).astype(BF16)
            send(
                qsend.at[ra - 1, pair(g)],
                r4.at[ra - 1, pair(g)],
                s4.at[0],
                r4s.at[ra - 1, g],
                apeer(ra),
            )

    def finish_a(g):
        total = summed_b(0, g)
        for i in range(3):
            arrived(r4.at[i, pair(g)], s4.at[0], r4s.at[i, g])
            total = total + r4[i, 2 * g : 2 * g + 2].astype(F32)
        outs[g, 0] = total.astype(BF16)
        send(outs.at[g, 0], outs.at[g, 1], out_s.at[0], out_r.at[g], sibling)

    def spread(g):
        arrived(outs.at[g, 1], out_s.at[0], out_r.at[g])
        given = (
            lax.dot_general(
                chooser[...],
                outs[g].reshape(TOK, W),
                (((0,), (0,)), ((), ())),
                preferred_element_type=F32,
            )
            * weight_col
        ).reshape(NZ, 16, W)
        upd16[g] = upd16[g] + given[0]
        csend[:, g] = given.astype(BF16)
        for i in far_first:
            send(csend.at[i, g], crecv.at[i, g], zs3.at[0], zr3.at[g], zpeer(RZ[i]))

    for g in range(NG):
        add_b(g)
    for turn in range(NG + 3):
        if turn < NG:
            start_a(turn)
        if 0 <= turn - 2 < NG:
            finish_a(turn - 2)
        if 0 <= turn - 3 < NG:
            spread(turn - 3)
    for g in range(NG):
        arrived(crecv.at[pl.ds(1, NZ - 1), g], zs3.at[0], zr3.at[g])
        total = upd16[g]
        for i in range(1, NZ):
            total = total + crecv[i, g].astype(F32)
        for f in range(2):
            out[:, (2 * g + f) * W : (2 * g + f + 1) * W] = total[8 * f : 8 * f + 8].astype(BF16)

    left(proj.at[pl.ds(0, CH)], wsend.at[0])
    left(up.at[:, pl.ds(0, FFL)], wsend.at[1])
    left(down.at[pl.ds(0, FFL)], wsend.at[2])
    for d in range(1, NCTX):

        @pl.when(c + d == NCTX - 1)
        def _():
            left(carry.at[pl.ds(0, d)], carry_s.at[0])
            left(sums.at[pl.ds(0, d)], sum_s.at[0])

    left(gsend, gate_s.at[0])
    left(rp0, p0_s.at[0])
    left(rp, p_s.at[0])
    left(rows.at[pl.ds(1, NZ - 1)], zs2.at[0])
    left(selsend, sel_s.at[0])
    left(x.at[pl.ds(0, 15)], ag_s.at[0])
    left(r1, s1.at[0])
    left(r2, s2.at[0])
    left(r4, s4.at[0])
    left(selsend, out_s.at[0])
    left(crecv.at[pl.ds(1, NZ - 1)], zs3.at[0])


def per_device(
    residual,
    mixer_input,
    mixer_gate,
    step_size,
    decay_rate,
    state_in,
    state_out,
    skip_weight,
    projection,
    norm_gain,
    routes,
    route_weight,
    up_weight,
    down_weight,
):
    vmem = pl.BlockSpec(memory_space=pltpu.VMEM)
    hbm = pl.BlockSpec(memory_space=pl.ANY)
    dma = pltpu.SemaphoreType.DMA
    scratch = [
        pltpu.VMEM((8, D), BF16),
        pltpu.VMEM((TOK, CH), BF16),
        pltpu.VMEM((TOK, CH), BF16),
        pltpu.VMEM((TOK, CH), F32),
        pltpu.VMEM((NS, CH), F32),
        pltpu.VMEM((NS, TOK), F32),
        pltpu.VMEM((NS, TOK), F32),
        pltpu.VMEM((2 * CH, D), BF16),
        pltpu.VMEM((D, 2 * FFL), BF16),
        pltpu.VMEM((2 * FFL, D), BF16),
        pltpu.VMEM((TOK, NS, CH), F32),
        pltpu.VMEM((TOK, CH), F32),
        pltpu.VMEM((TOK, CH), F32),
        pltpu.VMEM((NCTX, NS, CH), BF16),
        pltpu.VMEM((NCTX, 1, CH), F32),
        pltpu.VMEM((64, CH), BF16),
        pltpu.VMEM((64, CH), BF16),
        pltpu.VMEM((64, CH), BF16),
        pltpu.VMEM((NZ, NG, 16, W), BF16),
        pltpu.VMEM((2, 2, 16, W), BF16),
        pltpu.VMEM((2, 3, NG, 16, W), BF16),
        pltpu.VMEM((NG, 16, W), F32),
        pltpu.VMEM((NG, 16, W), F32),
        pltpu.VMEM((NZ, NG, 16, W), BF16),
        pltpu.VMEM((TOK, TOK), BF16),
        pltpu.VMEM((NG, 2, 32, W), BF16),
        pltpu.VMEM((NG, 2, 32, W), BF16),
        pltpu.VMEM((16, 2 * NG, 32, W), BF16),
        pltpu.VMEM((4, TOK, 2 * FFL), F32),
        pltpu.VMEM((TOK, 2 * FFL), BF16),
        pltpu.VMEM((4, 4, 2 * NG, 32, W), BF16),
        pltpu.VMEM((2, 4, NG, 32, W), BF16),
        pltpu.VMEM((2, 4, 2 * NG, 32, W), BF16),
        pltpu.VMEM((3, 2 * NG, 32, W), BF16),
        pltpu.VMEM((3, 2 * NG, 32, W), BF16),
        pltpu.VMEM((NG, 2, 2, 32, W), BF16),
        pltpu.VMEM((NZ, NG, 16, W), BF16),
        pltpu.VMEM((NZ, NG, 16, W), BF16),
        dma((7,)),
        dma((3,)),
        dma((3,)),
        dma((3,)),
        dma((1,)),
        dma((1,)),
        dma((1,)),
        dma((1,)),
        dma((1,)),
        dma((1,)),
        dma((1,)),
        dma((NG,)),
        dma((1,)),
        dma((NG,)),
        dma((1,)),
        dma((2,)),
        dma((1,)),
        dma((2, 3)),
        dma((1,)),
        dma((NG, 2)),
        dma((1,)),
        dma((NG,)),
        dma((1,)),
        dma((12, NG)),
        dma((4, 2 * NG)),
        dma((1,)),
        dma((2, NG)),
        dma((1,)),
        dma((2, NG)),
        dma((2, NG)),
        dma((1,)),
        dma((3, NG)),
    ]
    return pl.pallas_call(
        layer_kernel,
        out_shape=jax.ShapeDtypeStruct(residual.shape, BF16),
        in_specs=[
            hbm, hbm, hbm, hbm, hbm, hbm, hbm, vmem,
            hbm, vmem, vmem, vmem, hbm, hbm,
        ],
        out_specs=vmem,
        scratch_shapes=scratch,
        compiler_params=pltpu.CompilerParams(
            collective_id=0, has_side_effects=True, vmem_limit_bytes=58 * 1024 * 1024
        ),
    )(
        residual,
        mixer_input,
        mixer_gate,
        step_size,
        decay_rate,
        state_in.T,
        state_out.T,
        skip_weight.reshape(1, CH),
        projection,
        norm_gain.reshape(1, D),
        routes.T,
        route_weight.T,
        up_weight,
        down_weight,
    )


def solution(mesh):
    in_specs = (
        P(("ctx", "exp", "half"), None),
        P("ctx", ("exp", "half")),
        P("ctx", ("exp", "half")),
        P("ctx", ("exp", "half")),
        P(None, ("exp", "half")),
        P("ctx", None),
        P("ctx", None),
        P(("exp", "half")),
        P(("exp", "half"), None),
        P(),
        P("ctx", None),
        P("ctx", None),
        P("exp", None, ("ctx", "half")),
        P("exp", ("ctx", "half"), None),
    )
    out_specs = P(("ctx", "exp", "half"), None)
    return jax.shard_map(
        per_device, mesh=mesh, in_specs=in_specs, out_specs=out_specs, check_vma=False
    )
```

```python
import jax
import jax.numpy as jnp
from jax import lax
from jax.experimental import pallas as pl
from jax.experimental.pallas import tpu as pltpu
from jax.sharding import PartitionSpec as P

F32 = jnp.float32
BF16 = jnp.bfloat16
TOK = 128
CH = 512
NS = 16
D = 4096
FFL = 384
NZ = 8
NCTX = 16
NG = 4
AHEAD = 2
W = 512
RZ = (0, 1, 2, 7, 6, 3, 4, 5)


def layer_kernel(
    residual_hbm,
    xin_hbm,
    gate_hbm,
    step_hbm,
    rate_hbm,
    sin_hbm,
    sout_hbm,
    skip,
    proj_hbm,
    gain,
    routes,
    rweight,
    up_hbm,
    down_hbm,
    out,
    residual,
    xin,
    gate,
    step,
    rate,
    sin,
    sout,
    proj,
    up,
    down,
    dec,
    drive,
    yacc,
    carry,
    sums,
    gsend,
    gmine,
    gpeer,
    half,
    psend,
    rp0,
    rp,
    own16,
    upd16,
    rows,
    chooser,
    selsend,
    selpeer,
    x,
    pre,
    hid,
    part,
    r1,
    r2,
    r4,
    qsend,
    outs,
    csend,
    crecv,
    isem,
    wsem,
    wsend,
    wrecv,
    carry_s,
    carry_r,
    sum_s,
    sum_r,
    gate_s,
    gate_r,
    sel_s,
    sel_r,
    out_s,
    out_r,
    p0_s,
    p0_r,
    p_s,
    p_r,
    zs2,
    zr2,
    zs3,
    zr3,
    ag_s,
    ag_r,
    ag_half,
    s1,
    r1s,
    s2,
    r2early,
    r2late,
    s4,
    r4s,
):
    c = lax.axis_index("ctx")
    z = lax.axis_index("exp")
    h = lax.axis_index("half")
    def remote(src, dst, ssem, rsem, to):
        return pltpu.make_async_remote_copy(
            src_ref=src,
            dst_ref=dst,
            send_sem=ssem,
            recv_sem=rsem,
            device_id=to,
            device_id_type=pl.DeviceIdType.MESH,
        )

    def send(src, dst, ssem, rsem, to):
        remote(src, dst, ssem, rsem, to).start()

    sibling = {"ctx": c, "exp": z, "half": 1 - h}

    def arrived(dst, ssem, rsem):
        remote(dst, dst, ssem, rsem, sibling).wait_recv()

    def left(src, ssem):
        remote(src, src, ssem, ssem, sibling).wait_send()

    def zpeer(d):
        return {"ctx": c, "exp": lax.rem(z + d, NZ), "half": h}

    cy, cx = lax.div(c, 4), lax.rem(c, 4)
    a = cx + h * (cy - cx)
    b = cy + h * (cx - cy)

    def ctx_at(da, db):
        return lax.rem(a + da, 4) * (1 + 3 * h) + lax.rem(b + db, 4) * (4 - 3 * h)

    def apeer(d):
        return {"ctx": ctx_at(d, 0), "exp": z, "half": h}

    def bpeer(d):
        return {"ctx": ctx_at(0, d), "exp": z, "half": h}

    inputs = [
        pltpu.make_async_copy(src, dst, isem.at[i])
        for i, (src, dst) in enumerate(
            (
                (step_hbm, step),
                (xin_hbm, xin),
                (rate_hbm, rate),
                (sin_hbm, sin),
                (sout_hbm, sout),
                (gate_hbm, gate),
                (residual_hbm, residual),
            )
        )
    ]
    local = [
        pltpu.make_async_copy(proj_hbm, proj.at[pl.ds(0, CH)], wsem.at[0]),
        pltpu.make_async_copy(up_hbm.at[0], up.at[:, pl.ds(0, FFL)], wsem.at[1]),
        pltpu.make_async_copy(down_hbm.at[0], down.at[pl.ds(0, FFL)], wsem.at[2]),
    ]
    for copy in inputs + local:
        copy.start()

    barrier = pltpu.get_barrier_semaphore()
    for d in range(1, NCTX):
        pl.semaphore_signal(
            barrier,
            inc=1,
            device_id={"ctx": lax.rem(c + d, NCTX), "exp": z, "half": h},
            device_id_type=pl.DeviceIdType.MESH,
        )
    for d in range(1, NZ):
        pl.semaphore_signal(
            barrier, inc=1, device_id=zpeer(d), device_id_type=pl.DeviceIdType.MESH
        )
    pl.semaphore_signal(
        barrier, inc=1, device_id=sibling, device_id_type=pl.DeviceIdType.MESH
    )

    for copy in inputs:
        copy.wait()
    nrate = -rate[...]
    drive[...] = step[...] * xin[...].astype(F32)
    sums[c] = jnp.sum(step[...], axis=0, keepdims=True)

    def turned(ref, base):
        return pltpu.roll(ref[...], lax.rem(TOK - base, TOK), 1)

    def first_pass(tb, state):
        base = pl.multiple_of(tb * 8, 8)
        st8 = step[pl.ds(base, 8), :]
        dr8 = drive[pl.ds(base, 8), :]
        ins = turned(sin, base)
        for i in range(8):
            decay = jnp.exp(st8[i : i + 1, :] * nrate)
            dec[base + i] = decay
            state = decay * state + dr8[i : i + 1, :] * ins[:, i : i + 1]
        return state

    zero_state = jnp.zeros((NS, CH), F32)
    carry[c] = lax.fori_loop(0, TOK // 8, first_pass, zero_state).astype(BF16)

    pl.semaphore_wait(barrier, NCTX - 1 + NZ - 1 + 1)

    def later(d):
        return {"ctx": c + d, "exp": z, "half": h}

    for d in range(1, NCTX):

        @pl.when(c + d < NCTX)
        def _():
            remote(carry.at[c], carry.at[c], carry_s.at[0], carry_r.at[0], later(d)).start()
            remote(sums.at[c], sums.at[c], sum_s.at[0], sum_r.at[0], later(d)).start()

    send(proj_hbm, proj.at[pl.ds(CH, CH)], wsend.at[0], wrecv.at[0], sibling)

    hit0 = routes[0:1, :] == z
    hit1 = routes[1:2, :] == z
    hits = jnp.where(hit0 | hit1, 1.0, 0.0).astype(F32)
    weigh = jnp.where(hit0, rweight[0:1, :], 0.0) + jnp.where(hit1, rweight[1:2, :], 0.0)
    hits = jnp.broadcast_to(hits, (TOK, TOK)).T
    weigh = jnp.broadcast_to(weigh, (TOK, TOK)).T
    major = lax.broadcasted_iota(jnp.int32, (TOK, TOK), 0)
    minor = lax.broadcasted_iota(jnp.int32, (TOK, TOK), 1)
    place = minor >> 4
    place = jnp.where(place >= 5, place - 2, jnp.where(place >= 3, 10 - place, place))
    token = 16 * ((z + place) & 7) + 8 * h + (minor & 7)
    before = jnp.sum(jnp.where(major <= token, hits, 0.0), axis=0, keepdims=True)
    same = major == token
    named = jnp.sum(jnp.where(same, hits, 0.0), axis=0, keepdims=True)
    weight_row = jnp.sum(jnp.where(same, weigh, 0.0), axis=0, keepdims=True)
    who = major >> 6
    slot = 32 * (h + who * (1 - 2 * h)) + (major & 31)
    chosen = jnp.where(
        (((major >> 5) & 1) == ((minor >> 3) & 1)) & (before == (slot + 1).astype(F32)),
        named,
        0.0,
    )
    chooser[...] = chosen.astype(BF16)
    weight_col = jnp.broadcast_to(weight_row, (TOK, TOK)).T[:, 0:1]

    for d in range(1, NCTX):

        @pl.when(c == d)
        def _():
            arrived(carry.at[pl.ds(0, d)], carry_s.at[0], carry_r.at[0])
            arrived(sums.at[pl.ds(0, d)], sum_s.at[0], sum_r.at[0])

    def enter(j, state):
        return jnp.exp(sums[j] * nrate) * state + carry[j].astype(F32)

    entering = lax.fori_loop(0, c, enter, zero_state)

    def second_pass(tb, state):
        base = pl.multiple_of(tb * 8, 8)
        dr8 = drive[pl.ds(base, 8), :]
        ins = turned(sin, base)
        outw = turned(sout, base)
        for i in range(8):
            state = dec[base + i] * state + dr8[i : i + 1, :] * ins[:, i : i + 1]
            yacc[pl.ds(base + i, 1), :] = jnp.sum(
                state * outw[:, i : i + 1], axis=0, keepdims=True
            )
        return state

    lax.fori_loop(0, TOK // 8, second_pass, entering)

    gates = gate[...].astype(F32)
    yacc[...] = (yacc[...] + skip[...] * xin[...].astype(F32)) * (
        gates / (1.0 + jnp.exp(-gates))
    )

    def eights(whose):
        return jnp.concatenate(
            [
                yacc[pl.ds(pl.multiple_of(16 * lax.rem(z + d, NZ) + 8 * whose, 8), 8), :]
                for d in range(NZ)
            ],
            axis=0,
        ).astype(BF16)

    gsend[...] = eights(1 - h)
    send(gsend, gpeer, gate_s.at[0], gate_r.at[0], sibling)
    send(up_hbm.at[0], up.at[:, pl.ds(FFL, FFL)], wsend.at[1], wrecv.at[1], sibling)
    send(down_hbm.at[0], down.at[pl.ds(FFL, FFL)], wsend.at[2], wrecv.at[2], sibling)
    gmine[...] = eights(h)

    def columns(g, f):
        return pl.ds(pl.multiple_of((2 * g + f) * W, W), W)

    def project_mine(g, _):
        for f in range(2):
            half[g, f] = jnp.dot(
                gmine[...], proj[0:CH, columns(g, f)], preferred_element_type=F32
            )
        return 0

    def project(g, _):
        def block(f):
            return (
                half[g, f]
                + jnp.dot(
                    gpeer[...], proj[CH : 2 * CH, columns(g, f)], preferred_element_type=F32
                )
            ).reshape(NZ, 8, W)

        both = jnp.concatenate([block(0), block(1)], axis=1)
        own16[g] = both[0]
        psend[:, g] = both.astype(BF16)
        return 0

    local[0].wait()
    lax.fori_loop(0, NG, project_mine, 0)
    arrived(proj.at[pl.ds(CH, CH)], wsend.at[0], wrecv.at[0])
    arrived(gpeer, gate_s.at[0], gate_r.at[0])
    lax.fori_loop(0, NG, project, 0)

    for way in range(2):
        send(
            psend.at[4, pl.ds(2 * way, 2)],
            rp0.at[way],
            p0_s.at[0],
            p0_r.at[way],
            zpeer((2, 6)[way]),
        )
        send(psend.at[(3, 5)[way]], rp.at[way, 0], p_s.at[0], p_r.at[way, 0], zpeer((1, 7)[way]))
    for way in range(2):
        send(psend.at[(1, 7)[way]], rp.at[way, 1], p_s.at[0], p_r.at[way, 1], zpeer((1, 7)[way]))
    for way in range(2):
        pos = (2, 6)[way]
        arrived(rp.at[way, 0], p_s.at[0], p_r.at[way, 0])
        arrived(rp0.at[way], p0_s.at[0], p0_r.at[way])
        for g in range(NG):
            total = psend[pos, g].astype(F32) + rp[way, 0, g].astype(F32)
            if g // 2 == way:
                total = total + rp0[way, g % 2].astype(F32)
            psend[pos, g] = total.astype(BF16)
        send(psend.at[pos], rp.at[way, 2], p_s.at[0], p_r.at[way, 2], zpeer(pos))
    for way in range(2):
        for slot in (1, 2):
            arrived(rp.at[way, slot], p_s.at[0], p_r.at[way, slot])
    squares = jnp.zeros((16, 1), F32)
    for g in range(NG):
        res = residual[:, 2 * W * g : 2 * W * (g + 1)].astype(F32)
        total = own16[g] + jnp.concatenate([res[:, :W], res[:, W:]], axis=0)
        for way in range(2):
            total = total + rp[way, 1, g].astype(F32) + rp[way, 2, g].astype(F32)
        upd16[g] = total
        squares = squares + jnp.sum(total * total, axis=1, keepdims=True)

    scale = lax.rsqrt((squares[0:8] + squares[8:16]) * (1.0 / D) + 1e-05)
    scale = jnp.concatenate([scale, scale], axis=0)
    far_first = (6, 5, 7, 4, 2, 3, 1)

    def send_rows(g):
        for i in far_first:
            near = 0 if RZ.index(NZ - RZ[i]) < 5 else 1
            send(
                rows.at[0, g],
                rows.at[RZ.index(NZ - RZ[i]), g],
                zs2.at[0],
                zr2.at[g, near],
                zpeer(RZ[i]),
            )

    for g in range(NG):
        gains = jnp.concatenate(
            [
                jnp.broadcast_to(gain[:, (2 * g + f) * W : (2 * g + f + 1) * W], (8, W))
                for f in range(2)
            ],
            axis=0,
        )
        rows[0, g] = (upd16[g] * scale * gains).astype(BF16)
        if g < AHEAD:
            send_rows(g)

    def select(g):
        arrived(rows.at[pl.ds(1, 4), g], zs2.at[0], zr2.at[g, 0])
        if g + AHEAD < NG:
            send_rows(g + AHEAD)
        arrived(rows.at[pl.ds(5, 3), g], zs2.at[0], zr2.at[g, 1])
        picked = jnp.dot(
            chooser[...], rows[:, g].reshape(TOK, W), preferred_element_type=F32
        )
        selsend[g] = picked[64:128].astype(BF16).reshape(2, 32, W)
        send(selsend.at[g], selpeer.at[g], sel_s.at[0], sel_r.at[g], sibling)
        arrived(selpeer.at[g], sel_s.at[0], sel_r.at[g])
        x[0, 2 * g : 2 * g + 2] = (
            picked[0:64].reshape(2, 32, W) + selpeer[g].astype(F32)
        ).astype(BF16)

    def pair(g):
        return pl.ds(2 * g, 2)

    def ready(rb, ra, g):
        return ag_r.at[(8 if rb == 3 else 4 * rb) + ra, g]

    def gather(ra, g, to, lb, la):
        send(x.at[ra, pair(g)], x.at[4 * lb + la, pair(g)], ag_s.at[0], ready(lb, la, g), to)

    def have(rb, ra, g):
        arrived(x.at[4 * rb + ra, pair(g)], ag_s.at[0], ready(rb, ra, g))

    def along_b(ra, g):
        gather(ra, g, bpeer(1), 3, ra)
        gather(ra, g, bpeer(3), 1, ra)

    def begin(g):
        for d in (2, 1, 3):
            gather(0, g, apeer(d), 0, 4 - d)
        along_b(0, g)

    def neighbours(g):
        for ra in (3, 1, 2):
            have(0, ra, g)
            along_b(ra, g)

    def pass_on(g):
        for ra in (0, 3, 1, 2):
            for side in range(2):
                rb, e = 3 - 2 * side, 2 * g + side
                have(rb, ra, g)
                send(
                    x.at[4 * rb + ra, e],
                    x.at[8 + ra, e],
                    ag_s.at[0],
                    ag_half.at[ra, e],
                    bpeer(1 + 2 * side),
                )

    def widen(rb, g):
        wide = jnp.concatenate(
            [x[4 * rb : 4 * rb + 4, e].reshape(TOK, W) for e in (2 * g, 2 * g + 1)], axis=1
        )
        got = jnp.dot(wide, up[2 * g * W : 2 * (g + 1) * W, :], preferred_element_type=F32)
        if g == 0:
            pre[rb] = got
        elif g < NG - 1:
            pre[rb] = pre[rb] + got
        else:
            got = pre[rb] + got
            hid[...] = (got / (1.0 + jnp.exp(-got))).astype(BF16)

    for turn in range(NG):
        select(turn)
        begin(turn)
        if turn == 0:
            local[1].wait()
            local[2].wait()
            arrived(up.at[:, pl.ds(FFL, FFL)], wsend.at[1], wrecv.at[1])
            arrived(down.at[pl.ds(FFL, FFL)], wsend.at[2], wrecv.at[2])
        if turn >= 1:
            neighbours(turn - 1)
            widen(0, turn - 1)
        if turn >= 2:
            pass_on(turn - 2)
            widen(1, turn - 2)
            widen(3, turn - 2)
    neighbours(NG - 1)
    pass_on(NG - 2)

    def narrow(rb, g):
        for e in (2 * g, 2 * g + 1):
            part[rb, :, e] = (
                jnp.dot(hid[...], down[:, e * W : (e + 1) * W], preferred_element_type=F32)
                .astype(BF16)
                .reshape(4, 32, W)
            )

    widen(0, NG - 1)
    for g in range(NG):
        narrow(0, g)
    widen(1, NG - 2)
    widen(3, NG - 2)
    pass_on(NG - 1)
    for side in range(2):
        widen(1 + 2 * side, NG - 1)
        for g in range(NG):
            e = 2 * g + 1 - side
            narrow(1 + 2 * side, g)
            send(
                part.at[1 + 2 * side, pl.ds(0, 4), e],
                r2.at[side, pl.ds(0, 4), e],
                s2.at[0],
                r2early.at[side, g],
                bpeer(1 + 2 * side),
            )
    for g in range(NG):
        for ra in range(4):
            for e in (2 * g, 2 * g + 1):
                arrived(x.at[8 + ra, e], ag_s.at[0], ag_half.at[ra, e])
        widen(2, g)
    for g in range(NG):
        narrow(2, g)
        for side in range(2):
            send(
                part.at[2, pl.ds(0, 4), 2 * g + side],
                r1.at[side, pl.ds(0, 4), g],
                s1.at[0],
                r1s.at[side, g],
                bpeer(1 + 2 * side),
            )

    def add_b(g):
        for side in range(2):
            arrived(r1.at[side, pl.ds(0, 4), g], s1.at[0], r1s.at[side, g])
        for side in range(2):
            e = 2 * g + side
            part[1 + 2 * side, :, e] = (
                part[1 + 2 * side, :, e].astype(F32) + r1[side, :, g].astype(F32)
            ).astype(BF16)
            send(
                part.at[1 + 2 * side, pl.ds(0, 4), e],
                r2.at[side, pl.ds(0, 4), e],
                s2.at[0],
                r2late.at[side, g],
                bpeer(1 + 2 * side),
            )

    def summed_b(ra, g):
        total = part[0, ra, 2 * g : 2 * g + 2].astype(F32)
        for side in range(2):
            total = total + r2[side, ra, 2 * g : 2 * g + 2].astype(F32)
        return total

    def start_a(g):
        for side in range(2):
            e = 2 * g + 1 - side
            arrived(r2.at[side, pl.ds(0, 4), e], s2.at[0], r2early.at[side, g])
            e = 2 * g + side
            arrived(r2.at[side, pl.ds(0, 4), e], s2.at[0], r2late.at[side, g])
        for ra in (2, 1, 3):
            qsend[ra - 1, 2 * g : 2 * g + 2] = summed_b(ra, g).astype(BF16)
            send(
                qsend.at[ra - 1, pair(g)],
                r4.at[ra - 1, pair(g)],
                s4.at[0],
                r4s.at[ra - 1, g],
                apeer(ra),
            )

    def finish_a(g):
        total = summed_b(0, g)
        for i in range(3):
            arrived(r4.at[i, pair(g)], s4.at[0], r4s.at[i, g])
            total = total + r4[i, 2 * g : 2 * g + 2].astype(F32)
        outs[g, 0] = total.astype(BF16)
        send(outs.at[g, 0], outs.at[g, 1], out_s.at[0], out_r.at[g], sibling)

    def spread(g):
        arrived(outs.at[g, 1], out_s.at[0], out_r.at[g])
        given = (
            lax.dot_general(
                chooser[...],
                outs[g].reshape(TOK, W),
                (((0,), (0,)), ((), ())),
                preferred_element_type=F32,
            )
            * weight_col
        ).reshape(NZ, 16, W)
        upd16[g] = upd16[g] + given[0]
        csend[:, g] = given.astype(BF16)
        for i in far_first:
            send(csend.at[i, g], crecv.at[i, g], zs3.at[0], zr3.at[g], zpeer(RZ[i]))

    for g in range(NG):
        add_b(g)
    for turn in range(NG + 3):
        if turn < NG:
            start_a(turn)
        if 0 <= turn - 2 < NG:
            finish_a(turn - 2)
        if 0 <= turn - 3 < NG:
            spread(turn - 3)
    for g in range(NG):
        arrived(crecv.at[pl.ds(1, NZ - 1), g], zs3.at[0], zr3.at[g])
        total = upd16[g]
        for i in range(1, NZ):
            total = total + crecv[i, g].astype(F32)
        for f in range(2):
            out[:, (2 * g + f) * W : (2 * g + f + 1) * W] = total[8 * f : 8 * f + 8].astype(BF16)

    left(proj.at[pl.ds(0, CH)], wsend.at[0])
    left(up.at[:, pl.ds(0, FFL)], wsend.at[1])
    left(down.at[pl.ds(0, FFL)], wsend.at[2])
    for d in range(1, NCTX):

        @pl.when(c + d == NCTX - 1)
        def _():
            left(carry.at[pl.ds(0, d)], carry_s.at[0])
            left(sums.at[pl.ds(0, d)], sum_s.at[0])

    left(gsend, gate_s.at[0])
    left(rp0, p0_s.at[0])
    left(rp, p_s.at[0])
    left(rows.at[pl.ds(1, NZ - 1)], zs2.at[0])
    left(selsend, sel_s.at[0])
    left(x.at[pl.ds(0, 15)], ag_s.at[0])
    left(r1, s1.at[0])
    left(r2, s2.at[0])
    left(r4, s4.at[0])
    left(selsend, out_s.at[0])
    left(crecv.at[pl.ds(1, NZ - 1)], zs3.at[0])


def per_device(
    residual,
    mixer_input,
    mixer_gate,
    step_size,
    decay_rate,
    state_in,
    state_out,
    skip_weight,
    projection,
    norm_gain,
    routes,
    route_weight,
    up_weight,
    down_weight,
):
    vmem = pl.BlockSpec(memory_space=pltpu.VMEM)
    hbm = pl.BlockSpec(memory_space=pl.ANY)
    dma = pltpu.SemaphoreType.DMA
    scratch = [
        pltpu.VMEM((8, D), BF16),
        pltpu.VMEM((TOK, CH), BF16),
        pltpu.VMEM((TOK, CH), BF16),
        pltpu.VMEM((TOK, CH), F32),
        pltpu.VMEM((NS, CH), F32),
        pltpu.VMEM((NS, TOK), F32),
        pltpu.VMEM((NS, TOK), F32),
        pltpu.VMEM((2 * CH, D), BF16),
        pltpu.VMEM((D, 2 * FFL), BF16),
        pltpu.VMEM((2 * FFL, D), BF16),
        pltpu.VMEM((TOK, NS, CH), F32),
        pltpu.VMEM((TOK, CH), F32),
        pltpu.VMEM((TOK, CH), F32),
        pltpu.VMEM((NCTX, NS, CH), BF16),
        pltpu.VMEM((NCTX, 1, CH), F32),
        pltpu.VMEM((64, CH), BF16),
        pltpu.VMEM((64, CH), BF16),
        pltpu.VMEM((64, CH), BF16),
        pltpu.VMEM((NG, 2, 64, W), F32),
        pltpu.VMEM((NZ, NG, 16, W), BF16),
        pltpu.VMEM((2, 2, 16, W), BF16),
        pltpu.VMEM((2, 3, NG, 16, W), BF16),
        pltpu.VMEM((NG, 16, W), F32),
        pltpu.VMEM((NG, 16, W), F32),
        pltpu.VMEM((NZ, NG, 16, W), BF16),
        pltpu.VMEM((TOK, TOK), BF16),
        pltpu.VMEM((NG, 2, 32, W), BF16),
        pltpu.VMEM((NG, 2, 32, W), BF16),
        pltpu.VMEM((16, 2 * NG, 32, W), BF16),
        pltpu.VMEM((4, TOK, 2 * FFL), F32),
        pltpu.VMEM((TOK, 2 * FFL), BF16),
        pltpu.VMEM((4, 4, 2 * NG, 32, W), BF16),
        pltpu.VMEM((2, 4, NG, 32, W), BF16),
        pltpu.VMEM((2, 4, 2 * NG, 32, W), BF16),
        pltpu.VMEM((3, 2 * NG, 32, W), BF16),
        pltpu.VMEM((3, 2 * NG, 32, W), BF16),
        pltpu.VMEM((NG, 2, 2, 32, W), BF16),
        pltpu.VMEM((NZ, NG, 16, W), BF16),
        pltpu.VMEM((NZ, NG, 16, W), BF16),
        dma((7,)),
        dma((3,)),
        dma((3,)),
        dma((3,)),
        dma((1,)),
        dma((1,)),
        dma((1,)),
        dma((1,)),
        dma((1,)),
        dma((1,)),
        dma((1,)),
        dma((NG,)),
        dma((1,)),
        dma((NG,)),
        dma((1,)),
        dma((2,)),
        dma((1,)),
        dma((2, 3)),
        dma((1,)),
        dma((NG, 2)),
        dma((1,)),
        dma((NG,)),
        dma((1,)),
        dma((12, NG)),
        dma((4, 2 * NG)),
        dma((1,)),
        dma((2, NG)),
        dma((1,)),
        dma((2, NG)),
        dma((2, NG)),
        dma((1,)),
        dma((3, NG)),
    ]
    return pl.pallas_call(
        layer_kernel,
        out_shape=jax.ShapeDtypeStruct(residual.shape, BF16),
        in_specs=[
            hbm, hbm, hbm, hbm, hbm, hbm, hbm, vmem,
            hbm, vmem, vmem, vmem, hbm, hbm,
        ],
        out_specs=vmem,
        scratch_shapes=scratch,
        compiler_params=pltpu.CompilerParams(
            collective_id=0, has_side_effects=True, vmem_limit_bytes=58 * 1024 * 1024
        ),
    )(
        residual,
        mixer_input,
        mixer_gate,
        step_size,
        decay_rate,
        state_in.T,
        state_out.T,
        skip_weight.reshape(1, CH),
        projection,
        norm_gain.reshape(1, D),
        routes.T,
        route_weight.T,
        up_weight,
        down_weight,
    )


def solution(mesh):
    in_specs = (
        P(("ctx", "exp", "half"), None),
        P("ctx", ("exp", "half")),
        P("ctx", ("exp", "half")),
        P("ctx", ("exp", "half")),
        P(None, ("exp", "half")),
        P("ctx", None),
        P("ctx", None),
        P(("exp", "half")),
        P(("exp", "half"), None),
        P(),
        P("ctx", None),
        P("ctx", None),
        P("exp", None, ("ctx", "half")),
        P("exp", ("ctx", "half"), None),
    )
    out_specs = P(("ctx", "exp", "half"), None)
    return jax.shard_map(
        per_device, mesh=mesh, in_specs=in_specs, out_specs=out_specs, check_vma=False
    )
```
